32 devices in a mesh: page: 4 (over x, core), tensor: 8 (over z, y).
Axes of the slice: x: 2, y: 2, z: 4, core: 2. Of those that a mesh axis runs over, the one named last changes fastest.
Arguments:
- tokens: bfloat16 [512, 2560], P('tensor'), may hold values from -6 to 6
- norm_gain: float32 [2560], replicated, may hold values from 0.1 to 1.9
- w_query: bfloat16 [2560, 2560], P(None, 'tensor'), may hold values from -0.125 to 0.125
- w_keyvalue: bfloat16 [2560, 1280], P(None, 'tensor'), may hold values from -0.125 to 0.125
- cache: bfloat16 [32, 8, 128, 1280], P('page', 'tensor'), may hold values from -180 to 180, as said below
- page_count: int32 [4, 8], P('page', 'tensor'), may hold values from 1 to 8, as said below
- page_owner: int32 [32, 8], P('page', 'tensor'), may hold values from 0 to 63
- keep_rows: int32 [32, 8, 32], P('page', 'tensor'), may hold values from 0 to 127, as said below
- dest_slot: int32 [32, 8], P('page', 'tensor'), may hold values from 0 to 7, as said below
Outputs:
- attended: bfloat16 [512, 2560], P('tensor')
- compacted: bfloat16 [32, 8, 32, 1280], P('page', 'tensor')
The draws below stay inside these ranges and needn't reach their ends.
Inputs may be any that keep to these rules, and one draw needn't show every extreme that they name: `cache`: normal values within 4.5; keys may carry a row scale. `page_count`: in every tensor index some holder has all 8 slots live. `keep_rows`: distinct within each page. `dest_slot`: value q * 2 * 2 + c names position c of holder q (with 2 = 2, c = 0); the live slots of one holder and tensor index name distinct destinations, and every holder's first slot of a tensor index goes to position 0 of one common holder of that index.
All inputs are finite; a program needn't handle non-finite values.
Results may differ from the reference program's by a relative error of at most 0.012.
Values may be sent and summed in bfloat16 or wider, within the bound.
A program may use at most 64 MiB of HBM per device.

```python
import math
import jax
import jax.numpy as jnp
import numpy as np
from jax import lax

D = 2560
HEADS = 32
KV_HEADS = 8
HEAD_DIM = 80
RT = 64
SRC = 8
ROWS = 128
KEEP = 32
GROUPS = 8
HOLDERS = 4
REQUESTS = 512
SLOTS = 32
CAP = 2
DST = 8
KVW = 1280


def draw_cache(key, part):
    base = jnp.clip(jax.random.normal(key, (SLOTS, GROUPS, ROWS, KVW), jnp.float32), -4.5, 4.5)
    return base.astype(jnp.bfloat16)


def draw_page_count(key, part):
    first_draw = jax.random.randint(jax.random.fold_in(key, 1), (HOLDERS, GROUPS), 0, SRC)
    second_draw = jax.random.randint(jax.random.fold_in(key, 2), (HOLDERS, GROUPS), 0, SRC)
    counts = 1 + first_draw * (second_draw + SRC - 1) // max(2 * (SRC - 1), 1)
    busiest = jax.random.randint(jax.random.fold_in(key, 3), (GROUPS,), 0, HOLDERS)
    counts = jnp.where(jnp.arange(HOLDERS)[:, None] == busiest[None, :], SRC, counts)
    return counts.astype(jnp.int32)


def draw_keep_rows(key, part):
    noise = jax.random.randint(key, (SLOTS, GROUPS, ROWS), 0, 1 << 20)
    scores_int = noise * ROWS + jnp.arange(ROWS, dtype=jnp.int32)
    order = jnp.argsort(scores_int, axis=-1)
    return order[:, :, :KEEP].astype(jnp.int32)


def draw_dest_slot(key, part):
    common = jax.random.randint(jax.random.fold_in(key, 11), (GROUPS,), 0, HOLDERS)
    noise = jax.random.randint(jax.random.fold_in(key, 12), (HOLDERS, GROUPS, DST), 0, 1 << 20)
    pair_index = jnp.arange(DST, dtype=jnp.int32)
    pair_holder = pair_index // CAP
    pair_place = pair_index % CAP
    ranked = noise * DST + pair_index
    ranked = jnp.where(pair_holder[None, None, :] == common[None, :, None], pair_place[None, None, :] - CAP, ranked)
    order = jnp.argsort(ranked, axis=-1)[:, :, :SRC]
    return jnp.transpose(order, (0, 2, 1)).reshape(SLOTS, GROUPS).astype(jnp.int32)


def touch_ends(result, stream_key, smallest, high):
    shape = result.shape
    spot = [jax.random.randint(jax.random.fold_in(stream_key, axis), (), 0, shape[axis]) for axis in range(len(shape))]
    result = result.at[tuple(spot)].set(smallest)
    longest = shape.index(max(shape))
    spot[longest] = (spot[longest] + 1) % shape[longest]
    return result.at[tuple(spot)].set(high)


def level_of(rng, shape, cuts, smallest, high):
    gain, own = 1.0, jax.random.fold_in(rng, 6)
    for position, parts in cuts:
        draws = jnp.exp(jax.random.uniform(jax.random.fold_in(own, position), (parts,), jnp.float32, smallest / len(cuts), high / len(cuts)))
        gain = gain * jnp.repeat(draws, shape[position] // parts).reshape([-1 if axis == position else 1 for axis in range(len(shape))])
    return gain


def rank_bounds(amount, lean):
    loads = [(1 << 20) // math.isqrt(standing ** lean) + 1 for standing in range(1, amount + 1)]
    width = 1 + sum(loads) // (1 << 30)
    return np.cumsum(np.array([max(1, weight // width) for weight in loads]))


def ranked_ids(key, shape, count, slope):
    table = rank_bounds(count, slope)
    ticket = jax.random.randint(jax.random.fold_in(key, 1), shape, 0, int(table[count - 1]))
    standing = jnp.searchsorted(jnp.asarray(table, jnp.int32), ticket, side="right")
    return jax.random.permutation(jax.random.fold_in(key, 2), count)[standing].astype(jnp.int32)


def gaussian(rng, extent, deviation, bound, split=(), kind=jnp.bfloat16):
    values = jax.random.normal(rng, extent, jnp.float32) * deviation
    if len(split) > 0:
        values = level_of(rng, extent, split, -0.22, 0.18) * values
    return jnp.clip(values, min=-bound, max=bound).astype(kind)


def setup_inputs(seed: int = 0) -> dict:
    key_of = jax.random.split(jax.random.key(seed), 10)
    tokens = gaussian(key_of[0], (REQUESTS, D), 1.0, 6.0, ((0, 8),))
    norm_gain = jnp.clip(1.0 + 0.18 * jax.random.normal(key_of[1], (D,), jnp.float32), 0.1, 1.9)
    w_query = gaussian(key_of[2], (D, HEADS * HEAD_DIM), D ** -0.5, 0.125, ((1, 8),))
    w_keyvalue = gaussian(key_of[3], (D, KVW), D ** -0.5, 0.125, ((1, 8),))
    cache = draw_cache(jax.random.fold_in(key_of[9], 71), 0)
    page_count = draw_page_count(jax.random.fold_in(key_of[9], 71), 0)
    page_owner = touch_ends(ranked_ids(key_of[6], (SLOTS, GROUPS), RT, 2), jax.random.fold_in(key_of[6], 3), 0, RT - 1).astype(jnp.int32)
    keep_rows = draw_keep_rows(jax.random.fold_in(key_of[9], 71), 0)
    dest_slot = draw_dest_slot(jax.random.fold_in(key_of[9], 71), 0)
    return {"tokens": tokens, "norm_gain": norm_gain, "w_query": w_query, "w_keyvalue": w_keyvalue, "cache": cache, "page_count": page_count, "page_owner": page_owner, "keep_rows": keep_rows, "dest_slot": dest_slot}


EPSILON = 1e-05
NEGATIVE = -1e+30

def reference(tokens, norm_gain, w_query, w_keyvalue, cache, page_count, page_owner, keep_rows, dest_slot):
    widened = tokens.astype(jnp.float32)
    normed = (widened * lax.rsqrt(lax.optimization_barrier(jnp.mean(widened * widened, axis=-1, keepdims=True)) + EPSILON) * norm_gain).astype(jnp.bfloat16)
    queries = jnp.dot(normed, w_query, preferred_element_type=jnp.float32).astype(jnp.bfloat16)
    keyvalues = jnp.dot(normed, w_keyvalue, preferred_element_type=jnp.float32).astype(jnp.bfloat16)
    retained = jax.vmap(jax.vmap(lambda one_page, row_picks: one_page[row_picks]))(cache, keep_rows)
    slot_index = jnp.arange(SLOTS, dtype=jnp.int32)
    sender = slot_index // SRC
    is_live = (slot_index % SRC)[:, None] < page_count[sender]
    target = dest_slot // CAP * DST + sender[:, None] * CAP + dest_slot % CAP
    target = jnp.where(is_live, target, HOLDERS * DST).astype(jnp.int32)
    group_ids = jnp.broadcast_to(jnp.arange(GROUPS, dtype=jnp.int32)[None, :], target.shape)
    compacted = jnp.zeros((HOLDERS * DST, GROUPS, KEEP, KVW), cache.dtype).at[target, group_ids].set(retained, mode='drop')
    score_scale = HEAD_DIM ** (-0.5)
    repeat_count = HEADS // KV_HEADS

    def one_group(group_index):
        rows_q = lax.dynamic_slice_in_dim(queries, group_index * RT, RT, 0).astype(jnp.float32)
        rows_q = rows_q.reshape(RT, KV_HEADS, repeat_count, HEAD_DIM)
        rows_kv = lax.dynamic_slice_in_dim(keyvalues, group_index * RT, RT, 0).astype(jnp.float32)
        rows_kv = rows_kv.reshape(RT, 2, KV_HEADS, HEAD_DIM)
        group_pages = lax.dynamic_index_in_dim(retained, group_index, 1, keepdims=False).astype(jnp.float32)
        slot_keys = group_pages[:, :, :KV_HEADS * HEAD_DIM].reshape(SLOTS, KEEP, KV_HEADS, HEAD_DIM)
        slot_values = group_pages[:, :, KV_HEADS * HEAD_DIM:].reshape(SLOTS, KEEP, KV_HEADS, HEAD_DIM)
        owners = lax.dynamic_index_in_dim(page_owner, group_index, 1, keepdims=False)
        alive = lax.dynamic_index_in_dim(is_live, group_index, 1, keepdims=False)
        member = (owners[None, :] == jnp.arange(RT, dtype=jnp.int32)[:, None]) & alive[None, :]
        valid = member[:, None, None, :, None]
        scores = jnp.einsum('rgkd,sjgd->rgksj', rows_q, slot_keys) * score_scale
        own_score = jnp.einsum('rgkd,rgd->rgk', rows_q, rows_kv[:, 0]) * score_scale
        row_peak = jnp.maximum(lax.optimization_barrier(jnp.max(jnp.where(valid, scores, NEGATIVE), axis=(3, 4))), own_score)
        weights = jnp.where(valid, jnp.exp(scores - row_peak[..., None, None]), 0.0)
        own_weight = jnp.exp(own_score - row_peak)
        total = lax.optimization_barrier(jnp.sum(weights, axis=(3, 4))) + own_weight
        rounded = lax.optimization_barrier(weights.astype(jnp.bfloat16)).astype(jnp.float32)
        mixed = jnp.einsum('rgksj,sjgd->rgkd', rounded, slot_values)
        mixed = mixed + own_weight[..., None] * rows_kv[:, 1][:, :, None, :]
        return (mixed / total[..., None]).reshape(RT, HEADS * HEAD_DIM).astype(jnp.bfloat16)
    attended = lax.map(one_group, jnp.arange(GROUPS, dtype=jnp.int32)).reshape(REQUESTS, HEADS * HEAD_DIM)
    return (attended, compacted)
```

```python
import functools

import jax
import jax.numpy as jnp
from jax import lax
from jax.experimental import pallas as pl
from jax.experimental.pallas import tpu as pltpu
from jax.sharding import PartitionSpec as P

HEADS = 32
KV_HEADS = 8
HEAD_DIM = 80


EPSILON = 1e-05
NEGATIVE = -1e30


def per_device(
    tokens, norm_gain, w_query, w_keyvalue, cache, page_count, page_owner, keep_rows, dest_slot
):
    holders = lax.axis_size("page")
    groups = lax.axis_size("tensor")
    rows_here = tokens.shape[0]
    sources = cache.shape[0]
    keep_count = keep_rows.shape[2]
    row_width = cache.shape[3]
    capacity = (sources + holders - 1) // holders
    targets = capacity * holders
    repeat_count = HEADS // KV_HEADS
    score_scale = HEAD_DIM ** (-0.5)
    widened = tokens.astype(jnp.float32)
    normed = (
        widened
        * lax.rsqrt(jnp.mean(widened * widened, axis=-1, keepdims=True) + EPSILON)
        * norm_gain
    ).astype(jnp.bfloat16)
    portion = lax.all_gather(normed, "tensor", axis=0, tiled=True)
    query_part = jnp.dot(portion, w_query, preferred_element_type=jnp.float32)
    pair_part = jnp.dot(portion, w_keyvalue, preferred_element_type=jnp.float32)
    projected = jnp.concatenate([query_part, pair_part], axis=1).astype(jnp.bfloat16)
    local_heads = lax.all_to_all(
        projected, "tensor", split_axis=0, concat_axis=1, tiled=True
    ).reshape(rows_here, groups, -1)
    query_cols = w_query.shape[1]
    queries = local_heads[:, :, :query_cols].reshape(rows_here, KV_HEADS, repeat_count, HEAD_DIM)
    fresh_kv = local_heads[:, :, query_cols:].reshape(rows_here, 2, KV_HEADS, HEAD_DIM)
    new_keys = fresh_kv[:, 0]
    new_values = fresh_kv[:, 1]
    retained = jax.vmap(lambda one_page, row_picks: one_page[row_picks])(
        cache[:, 0], keep_rows[:, 0]
    )
    is_live = jnp.arange(sources) < page_count[0, 0]
    owners = page_owner[:, 0]
    chosen = (dest_slot[:, 0][None, :] == jnp.arange(targets)[:, None]) & is_live[None, :]
    outgoing = jnp.einsum(
        "ts,sjc->tjc", chosen.astype(jnp.bfloat16), retained, preferred_element_type=jnp.float32
    ).astype(jnp.bfloat16)
    out_tags = jnp.sum(jnp.where(chosen, owners[None, :] + 1, 0), axis=1) - 1
    arrived, arrived_tags = (
        lax.all_to_all(
            outgoing.reshape(holders, capacity, keep_count, row_width),
            "page",
            split_axis=0,
            concat_axis=0,
            tiled=True,
        ),
        lax.all_to_all(
            out_tags.reshape(holders, capacity), "page", split_axis=0, concat_axis=0, tiled=True
        ),
    )
    arrived = arrived.reshape(targets, keep_count, row_width)
    arrived_tags = arrived_tags.reshape(targets)
    slot_count = arrived.shape[0]
    active = arrived_tags >= 0
    owner_idx = jnp.maximum(arrived_tags, 0)
    picked = jnp.take(queries, owner_idx, axis=0)
    slot_keys = arrived[:, :, : KV_HEADS * HEAD_DIM].reshape(
        slot_count, keep_count, KV_HEADS, HEAD_DIM
    )
    slot_values = arrived[:, :, KV_HEADS * HEAD_DIM :].reshape(
        slot_count, keep_count, KV_HEADS, HEAD_DIM
    )
    scores = (
        jnp.einsum("sgkd,sjgd->sgkj", picked, slot_keys, preferred_element_type=jnp.float32)
        * score_scale
    )
    member = (owner_idx[None, :] == jnp.arange(rows_here)[:, None]) & active[None, :]
    slot_peak = jnp.max(scores, axis=3)
    local_peak = jnp.max(jnp.where(member[:, :, None, None], slot_peak[None], NEGATIVE), axis=1)
    own_score = (
        jnp.einsum("rgkd,rgd->rgk", queries, new_keys, preferred_element_type=jnp.float32)
        * score_scale
    )
    row_peak = jnp.maximum(lax.pmax(local_peak, "page"), own_score)
    shifted = scores - jnp.take(row_peak, owner_idx, axis=0)[..., None]
    weights = jnp.where(active[:, None, None, None], jnp.exp(shifted), 0.0)
    slot_total = jnp.sum(weights, axis=3)
    slot_out = jnp.einsum(
        "sgkj,sjgd->sgkd",
        weights.astype(jnp.bfloat16),
        slot_values,
        preferred_element_type=jnp.float32,
    )
    member_weight = member.astype(jnp.float32)
    part_total = jnp.einsum(
        "rs,sgk->rgk", member_weight, slot_total, precision=lax.Precision.HIGHEST
    )
    part_out = jnp.einsum("rs,sgkd->rgkd", member_weight, slot_out, precision=lax.Precision.HIGHEST)
    sum_out, sum_total = lax.psum((part_out, part_total), "page")
    own_weight = jnp.exp(own_score - row_peak)
    mixed = sum_out + own_weight[..., None] * new_values[:, :, None, :].astype(jnp.float32)
    result = mixed / (sum_total + own_weight)[..., None]
    return (result.reshape(rows_here, HEADS * HEAD_DIM).astype(jnp.bfloat16), arrived[:, None])


MESH = pl.DeviceIdType.MESH
SCALE = HEAD_DIM ** (-0.5)
REPEAT = HEADS // KV_HEADS
PLANE = KV_HEADS * HEAD_DIM
HOLDERS, GROUPS = 4, 8


def head_of(shape, axis):
    return (lax.broadcasted_iota(jnp.int32, shape, axis) * 3277) >> 18


def partner(index, flip):
    for bit in (1, 2, 4):
        if flip & bit:
            index = index + bit - 2 * bit * lax.rem(lax.div(index, bit), 2)
    return index


def split_dot(a, b):
    high = a.astype(jnp.bfloat16)
    low = (a - high.astype(jnp.float32)).astype(jnp.bfloat16)
    return jnp.dot(high, b, preferred_element_type=jnp.float32) + jnp.dot(
        low, b, preferred_element_type=jnp.float32
    )


def exact_dot(a, b):
    return jnp.dot(a, b, precision=lax.Precision.HIGHEST, preferred_element_type=jnp.float32)


def fused_kernel(
    tokens, gain, code, tags, tag_rows, w_query, w_keyvalue, cache,
    attended, compacted,
    wq, wkv, pages, rows, leaving, projected, local, planes, fresh, sums, peaks,
    load_sem, keep_sem, row_send, row_recv, page_send, page_recv, proj_send, proj_recv,
    query_send, query_recv, fresh_send, fresh_recv, sum_send, sum_recv, peak_send, peak_recv,
):
    p = lax.axis_index("page")
    t = lax.axis_index("tensor")
    part = rows.shape[1]
    requests = part * HOLDERS
    slots = tags.shape[0]
    keep = leaving.shape[1]
    cap = slots // HOLDERS
    page_rows = cache.shape[0] // slots

    loads = [
        pltpu.make_async_copy(cache, pages, load_sem.at[0]),
        pltpu.make_async_copy(w_query, wq, load_sem.at[1]),
        pltpu.make_async_copy(w_keyvalue, wkv, load_sem.at[2]),
    ]
    for load in loads:
        load.start()

    barrier = pltpu.get_barrier_semaphore()
    for f in range(1, GROUPS):
        pl.semaphore_signal(barrier, inc=1, device_id=(p, partner(t, f)), device_id_type=MESH)
    for f in range(1, HOLDERS):
        pl.semaphore_signal(barrier, inc=1, device_id=(partner(p, f), t), device_id_type=MESH)

    mine = tokens[p].astype(jnp.float32)
    square = jnp.mean(mine * mine, axis=-1, keepdims=True)
    rows[0] = (mine * lax.rsqrt(square + EPSILON) * gain[...]).astype(jnp.bfloat16)
    pl.semaphore_wait(barrier, GROUPS + HOLDERS - 2)

    def pass_row(e, f):
        copy = pltpu.make_async_remote_copy(
            src_ref=rows.at[e],
            dst_ref=rows.at[e ^ f],
            send_sem=row_send.at[e ^ f],
            recv_sem=row_recv.at[e ^ f],
            device_id=(p, partner(t, f)),
            device_id_type=MESH,
        )
        copy.start()
        return copy

    moved = {4: pass_row(0, 4), 2: pass_row(0, 2), 1: pass_row(0, 1)}

    loads[0].wait()
    lane = lax.broadcasted_iota(jnp.int32, (slots * keep, page_rows), 1)
    code_values = code[...]
    choice = jnp.concatenate(
        [jnp.where(code_values[:, s : s + 1] == lane, 1.0, 0.0).astype(jnp.bfloat16) for s in range(slots)],
        axis=1,
    )
    out = jnp.dot(choice, pages[...], preferred_element_type=jnp.float32).astype(jnp.bfloat16)
    leaving[...] = out.reshape(leaving.shape)
    page_copies = []
    for f in range(1, HOLDERS):
        copy = pltpu.make_async_remote_copy(
            src_ref=leaving.at[pl.ds(partner(p, f) * cap, cap)],
            dst_ref=compacted.at[pl.ds(p * cap, cap)],
            send_sem=page_send.at[f],
            recv_sem=page_recv.at[f],
            device_id=(partner(p, f), t),
            device_id_type=MESH,
        )
        copy.start()
        page_copies.append(copy)
    kept = pltpu.make_async_copy(
        leaving.at[pl.ds(p * cap, cap)], compacted.at[pl.ds(p * cap, cap)], keep_sem
    )
    kept.start()

    moved[4].wait_recv()
    moved[6] = pass_row(4, 2)
    moved[5] = pass_row(4, 1)
    moved[2].wait_recv()
    moved[3] = pass_row(2, 1)
    loads[1].wait()
    loads[2].wait()
    moved[6].wait_recv()
    moved[7] = pass_row(6, 1)

    def project(first):
        batch = jnp.concatenate([rows[e] for e in range(first, GROUPS, 2)], axis=0)
        query = jnp.dot(batch, wq[...], preferred_element_type=jnp.float32)
        pair = jnp.dot(batch, wkv[...], preferred_element_type=jnp.float32)
        spare = jnp.zeros((batch.shape[0], projected.shape[2] - 480), jnp.float32)
        both = jnp.concatenate([query, pair, spare], axis=1).astype(jnp.bfloat16)
        copies = []
        for n, e in enumerate(range(first, GROUPS, 2)):
            block = both[n * part : (n + 1) * part]
            if e == 0:
                local[t] = block
                continue
            projected[e] = block
            copy = pltpu.make_async_remote_copy(
                src_ref=projected.at[e],
                dst_ref=local.at[t],
                send_sem=proj_send.at[e],
                recv_sem=proj_recv.at[e],
                device_id=(p, partner(t, e)),
                device_id_type=MESH,
            )
            copy.start()
            copies.append(copy)
        return copies

    proj_copies = project(0)
    for e in (1, 3, 5, 7):
        moved[e].wait_recv()
    proj_copies += project(1)
    for copy in proj_copies:
        copy.wait_recv()

    blocks = [local[g].astype(jnp.float32) for g in range(GROUPS)]
    for k in range(REPEAT):
        planes[p, k] = jnp.concatenate(
            [b[:, k * HEAD_DIM : (k + 1) * HEAD_DIM] for b in blocks], axis=1
        ).astype(jnp.bfloat16)
    for n in range(2):
        fresh[p, n] = jnp.concatenate(
            [b[:, 320:480] for b in blocks[4 * n : 4 * n + 4]], axis=1
        ).astype(jnp.bfloat16)

    def to_holders(ref_of, send, recv):
        copies = []
        for f in range(1, HOLDERS):
            copy = pltpu.make_async_remote_copy(
                src_ref=ref_of(),
                dst_ref=ref_of(),
                send_sem=send.at[f],
                recv_sem=recv.at[f],
                device_id=(partner(p, f), t),
                device_id_type=MESH,
            )
            copy.start()
            copies.append(copy)
        return copies

    query_copies = to_holders(lambda: planes.at[p], query_send, query_recv)
    fresh_copies = to_holders(lambda: fresh.at[p], fresh_send, fresh_recv)

    def plane(ref, k):
        return jnp.concatenate([ref[h, k] for h in range(HOLDERS)], axis=0)

    pairs = slots * KV_HEADS
    member_row = jnp.where(
        tag_rows[...] == lax.broadcasted_iota(jnp.int32, (pairs, requests), 1).astype(jnp.float32),
        1.0,
        0.0,
    ).astype(jnp.bfloat16)
    own_head = head_of((pairs, PLANE), 1) == (
        lax.broadcasted_iota(jnp.int32, (pairs, PLANE), 0) & (KV_HEADS - 1)
    )
    slot_rows = leaving[...].reshape(slots * keep, 2 * PLANE)
    for copy in query_copies:
        copy.wait_recv()

    spread = []
    for k in range(REPEAT):
        q = plane(planes, k)
        found = jnp.dot(member_row, q, preferred_element_type=jnp.float32)
        spread.append(jnp.where(own_head, found, 0.0).astype(jnp.bfloat16))
    scores = SCALE * lax.dot_general(
        jnp.concatenate(spread, axis=0),
        slot_rows[:, :PLANE],
        (((1,), (1,)), ((), ())),
        preferred_element_type=jnp.float32,
    )
    full = (REPEAT * pairs, slots * keep)
    same = ((lax.broadcasted_iota(jnp.int32, full, 0) >> 3) & (slots - 1)) == (
        lax.broadcasted_iota(jnp.int32, full, 1) >> 5
    )
    scores = jnp.where(same, scores, NEGATIVE)
    peak = jnp.max(scores, axis=1, keepdims=True)
    weights = jnp.where(same, jnp.exp(scores - peak), 0.0)
    total = jnp.sum(weights, axis=1, keepdims=True)
    mixed = jnp.dot(
        weights.astype(jnp.bfloat16), slot_rows[:, PLANE:], preferred_element_type=jnp.float32
    ) / total
    mixed = mixed.reshape(REPEAT, pairs, PLANE)
    mixed = jnp.where(own_head[None], mixed, 0.0)
    mixed = jnp.sum(mixed.reshape(REPEAT * slots, KV_HEADS, PLANE), axis=1)
    sums[p] = mixed.astype(jnp.bfloat16)
    lse = peak + jnp.log(total)
    wide = (REPEAT * pairs, 128)
    row_id = lax.broadcasted_iota(jnp.int32, wide, 0)
    at = (row_id >> 6) * KV_HEADS + (row_id & (KV_HEADS - 1))
    lse = jnp.where(lax.broadcasted_iota(jnp.int32, wide, 1) == at, lse, 0.0)
    lse = jnp.sum(lse.reshape(REPEAT, slots, KV_HEADS, 128), axis=2)
    lse = lse[0] + lse[1] + lse[2] + lse[3]
    peaks[p] = jnp.where(
        lax.broadcasted_iota(jnp.int32, (slots, 128), 1) == 127, tags[...], lse
    )
    peak_copies = to_holders(lambda: peaks.at[p], peak_send, peak_recv)
    sum_copies = to_holders(lambda: sums.at[p], sum_send, sum_recv)

    for copy in fresh_copies:
        copy.wait_recv()
    new_keys = plane(fresh, 0).astype(jnp.float32)
    new_values = plane(fresh, 1).astype(jnp.float32)
    own = jnp.zeros((requests, 128), jnp.float32)
    segment_head = head_of((PLANE, 128), 0)
    segment_lane = lax.broadcasted_iota(jnp.int32, (PLANE, 128), 1)
    for k in range(REPEAT):
        q = plane(planes, k).astype(jnp.float32)
        segment = jnp.where(segment_lane == segment_head + k * KV_HEADS, 1.0, 0.0)
        own += split_dot(q * new_keys, segment.astype(jnp.bfloat16))
    own = own * SCALE

    for copy in peak_copies:
        copy.wait_recv()
    every = HOLDERS * slots
    lse = peaks[...].reshape(every, 128)
    owner = lse[:, 127:128]
    where_slot = lax.broadcasted_iota(jnp.int32, (every, every), 0)
    where_lane = lax.broadcasted_iota(jnp.int32, (every, every), 1)
    owner_row = jnp.sum(jnp.where(where_slot == where_lane, owner, 0.0), axis=0, keepdims=True)
    request = lax.broadcasted_iota(jnp.int32, (requests, every), 0).astype(jnp.float32)
    member = jnp.where(request == owner_row, 1.0, 0.0)
    request = lax.broadcasted_iota(jnp.int32, (every, requests), 1).astype(jnp.float32)
    slot_member = jnp.where(request == owner, 1.0, 0.0)
    top = own
    for s in range(every):
        top = jnp.maximum(top, jnp.where(member[:, s : s + 1] > 0.0, lse[s : s + 1], NEGATIVE))
    factor = jnp.exp(lse - exact_dot(slot_member, top))
    factor = jnp.where(owner >= 0.0, factor, 0.0)
    own_weight = jnp.exp(own - top)
    whole = exact_dot(member, factor) + own_weight
    slot_whole = exact_dot(slot_member, whole)
    slot_part = factor / jnp.where(owner >= 0.0, slot_whole, 1.0)
    own_part = own_weight / whole
    parts = jnp.concatenate([slot_part, own_part], axis=0)

    for copy in sum_copies:
        copy.wait_recv()
    slot_sums = sums[...].astype(jnp.float32).reshape(HOLDERS, REPEAT, slots, PLANE)
    member = member.astype(jnp.bfloat16)
    spread_head = head_of((128, PLANE), 1)
    spread_row = lax.broadcasted_iota(jnp.int32, (128, PLANE), 0)
    results = []
    for k in range(REPEAT):
        expand = jnp.where(spread_row == spread_head + k * KV_HEADS, 1.0, 0.0)
        shares = split_dot(parts, expand.astype(jnp.bfloat16))
        weighted = (shares[:every] * slot_sums[:, k].reshape(every, PLANE)).astype(jnp.bfloat16)
        results.append(
            jnp.dot(member, weighted, preferred_element_type=jnp.float32)
            + shares[every:] * new_values
        )
    attended[...] = jnp.concatenate(
        [
            results[k][:, g * HEAD_DIM : (g + 1) * HEAD_DIM]
            for g in range(KV_HEADS)
            for k in range(REPEAT)
        ],
        axis=1,
    ).astype(jnp.bfloat16)

    for copy in page_copies:
        copy.wait_recv()
    kept.wait()
    for copy in (
        list(moved.values()) + page_copies + proj_copies + query_copies + fresh_copies
        + peak_copies + sum_copies
    ):
        copy.wait_send()


def fused_device(
    tokens, norm_gain, w_query, w_keyvalue, cache, page_count, page_owner, keep_rows, dest_slot
):
    slots, _, page_rows, width = cache.shape
    keep = keep_rows.shape[2]
    requests, model = tokens.shape
    part = requests // HOLDERS
    is_live = jnp.arange(slots) < page_count[0, 0]
    chosen = (dest_slot[:, 0][None, :] == jnp.arange(slots)[:, None]) & is_live[None, :]
    code = jnp.where(chosen[:, None, :], keep_rows[:, 0].T[None], -1).reshape(slots * keep, slots)
    tags = jnp.sum(jnp.where(chosen, page_owner[:, 0][None, :] + 1, 0), axis=1) - 1
    tags = tags.astype(jnp.float32)
    vmem = pl.BlockSpec(memory_space=pltpu.VMEM)
    anywhere = pl.BlockSpec(memory_space=pl.ANY)
    bf16, f32 = jnp.bfloat16, jnp.float32
    dma = pltpu.SemaphoreType.DMA
    attended, compacted = pl.pallas_call(
        fused_kernel,
        out_shape=(
            jax.ShapeDtypeStruct((requests, HEADS * HEAD_DIM), bf16),
            jax.ShapeDtypeStruct((slots, keep, width), bf16),
        ),
        in_specs=[vmem] * 5 + [anywhere] * 3,
        out_specs=(vmem, anywhere),
        scratch_shapes=[
            pltpu.VMEM(w_query.shape, bf16),
            pltpu.VMEM(w_keyvalue.shape, bf16),
            pltpu.VMEM((slots * page_rows, width), bf16),
            pltpu.VMEM((GROUPS, part, model), bf16),
            pltpu.VMEM((slots, keep, width), bf16),
            pltpu.VMEM((GROUPS, part, 512), bf16),
            pltpu.VMEM((GROUPS, part, 512), bf16),
            pltpu.VMEM((HOLDERS, REPEAT, part, PLANE), bf16),
            pltpu.VMEM((HOLDERS, 2, part, PLANE), bf16),
            pltpu.VMEM((HOLDERS, REPEAT * slots, PLANE), bf16),
            pltpu.VMEM((HOLDERS, slots, 128), f32),
            dma((3,)),
            dma,
            dma((GROUPS,)),
            dma((GROUPS,)),
            dma((HOLDERS,)),
            dma((HOLDERS,)),
            dma((GROUPS,)),
            dma((GROUPS,)),
        ]
        + [dma((HOLDERS,))] * 8,
        compiler_params=pltpu.CompilerParams(
            collective_id=0, has_side_effects=True, vmem_limit_bytes=48 * 1024 * 1024
        ),
        cost_estimate=pl.CostEstimate(
            flops=1_500_000_000, bytes_accessed=7_000_000, transcendentals=70_000
        ),
    )(
        tokens.reshape(HOLDERS, part, model),
        norm_gain.reshape(1, model),
        code,
        tags.reshape(slots, 1),
        jnp.repeat(tags, KV_HEADS).reshape(slots * KV_HEADS, 1),
        w_query,
        w_keyvalue,
        cache.reshape(slots * page_rows, width),
    )
    return attended, compacted[:, None]


def local_step(sizes, tokens, norm_gain, w_query, w_keyvalue, cache, *rest):
    fits = (
        sizes == {"page": HOLDERS, "tensor": GROUPS}
        and tokens.shape[0] == 64
        and cache.shape[0] == 8
        and rest[2].shape[2] == 32
    )
    step = fused_device if fits else per_device
    return step(tokens, norm_gain, w_query, w_keyvalue, cache, *rest)


def solution(mesh):
    return jax.shard_map(
        functools.partial(local_step, dict(mesh.shape)),
        mesh=mesh,
        in_specs=(
            P("tensor", None),
            P(),
            P(None, "tensor"),
            P(None, "tensor"),
            P("page", "tensor", None, None),
            P("page", "tensor"),
            P("page", "tensor"),
            P("page", "tensor", None),
            P("page", "tensor"),
        ),
        out_specs=(P("tensor", None), P("page", "tensor", None, None)),
        check_vma=False,
    )
```

```python
import functools

import jax
import jax.numpy as jnp
from jax import lax
from jax.experimental import pallas as pl
from jax.experimental.pallas import tpu as pltpu
from jax.sharding import PartitionSpec as P

HEADS = 32
KV_HEADS = 8
HEAD_DIM = 80


EPSILON = 1e-05
NEGATIVE = -1e30


def per_device(
    tokens, norm_gain, w_query, w_keyvalue, cache, page_count, page_owner, keep_rows, dest_slot
):
    holders = lax.axis_size("page")
    groups = lax.axis_size("tensor")
    rows_here = tokens.shape[0]
    sources = cache.shape[0]
    keep_count = keep_rows.shape[2]
    row_width = cache.shape[3]
    capacity = (sources + holders - 1) // holders
    targets = capacity * holders
    repeat_count = HEADS // KV_HEADS
    score_scale = HEAD_DIM ** (-0.5)
    widened = tokens.astype(jnp.float32)
    normed = (
        widened
        * lax.rsqrt(jnp.mean(widened * widened, axis=-1, keepdims=True) + EPSILON)
        * norm_gain
    ).astype(jnp.bfloat16)
    portion = lax.all_gather(normed, "tensor", axis=0, tiled=True)
    query_part = jnp.dot(portion, w_query, preferred_element_type=jnp.float32)
    pair_part = jnp.dot(portion, w_keyvalue, preferred_element_type=jnp.float32)
    projected = jnp.concatenate([query_part, pair_part], axis=1).astype(jnp.bfloat16)
    local_heads = lax.all_to_all(
        projected, "tensor", split_axis=0, concat_axis=1, tiled=True
    ).reshape(rows_here, groups, -1)
    query_cols = w_query.shape[1]
    queries = local_heads[:, :, :query_cols].reshape(rows_here, KV_HEADS, repeat_count, HEAD_DIM)
    fresh_kv = local_heads[:, :, query_cols:].reshape(rows_here, 2, KV_HEADS, HEAD_DIM)
    new_keys = fresh_kv[:, 0]
    new_values = fresh_kv[:, 1]
    retained = jax.vmap(lambda one_page, row_picks: one_page[row_picks])(
        cache[:, 0], keep_rows[:, 0]
    )
    is_live = jnp.arange(sources) < page_count[0, 0]
    owners = page_owner[:, 0]
    chosen = (dest_slot[:, 0][None, :] == jnp.arange(targets)[:, None]) & is_live[None, :]
    outgoing = jnp.einsum(
        "ts,sjc->tjc", chosen.astype(jnp.bfloat16), retained, preferred_element_type=jnp.float32
    ).astype(jnp.bfloat16)
    out_tags = jnp.sum(jnp.where(chosen, owners[None, :] + 1, 0), axis=1) - 1
    arrived, arrived_tags = (
        lax.all_to_all(
            outgoing.reshape(holders, capacity, keep_count, row_width),
            "page",
            split_axis=0,
            concat_axis=0,
            tiled=True,
        ),
        lax.all_to_all(
            out_tags.reshape(holders, capacity), "page", split_axis=0, concat_axis=0, tiled=True
        ),
    )
    arrived = arrived.reshape(targets, keep_count, row_width)
    arrived_tags = arrived_tags.reshape(targets)
    slot_count = arrived.shape[0]
    active = arrived_tags >= 0
    owner_idx = jnp.maximum(arrived_tags, 0)
    picked = jnp.take(queries, owner_idx, axis=0)
    slot_keys = arrived[:, :, : KV_HEADS * HEAD_DIM].reshape(
        slot_count, keep_count, KV_HEADS, HEAD_DIM
    )
    slot_values = arrived[:, :, KV_HEADS * HEAD_DIM :].reshape(
        slot_count, keep_count, KV_HEADS, HEAD_DIM
    )
    scores = (
        jnp.einsum("sgkd,sjgd->sgkj", picked, slot_keys, preferred_element_type=jnp.float32)
        * score_scale
    )
    member = (owner_idx[None, :] == jnp.arange(rows_here)[:, None]) & active[None, :]
    slot_peak = jnp.max(scores, axis=3)
    local_peak = jnp.max(jnp.where(member[:, :, None, None], slot_peak[None], NEGATIVE), axis=1)
    own_score = (
        jnp.einsum("rgkd,rgd->rgk", queries, new_keys, preferred_element_type=jnp.float32)
        * score_scale
    )
    row_peak = jnp.maximum(lax.pmax(local_peak, "page"), own_score)
    shifted = scores - jnp.take(row_peak, owner_idx, axis=0)[..., None]
    weights = jnp.where(active[:, None, None, None], jnp.exp(shifted), 0.0)
    slot_total = jnp.sum(weights, axis=3)
    slot_out = jnp.einsum(
        "sgkj,sjgd->sgkd",
        weights.astype(jnp.bfloat16),
        slot_values,
        preferred_element_type=jnp.float32,
    )
    member_weight = member.astype(jnp.float32)
    part_total = jnp.einsum(
        "rs,sgk->rgk", member_weight, slot_total, precision=lax.Precision.HIGHEST
    )
    part_out = jnp.einsum("rs,sgkd->rgkd", member_weight, slot_out, precision=lax.Precision.HIGHEST)
    sum_out, sum_total = lax.psum((part_out, part_total), "page")
    own_weight = jnp.exp(own_score - row_peak)
    mixed = sum_out + own_weight[..., None] * new_values[:, :, None, :].astype(jnp.float32)
    result = mixed / (sum_total + own_weight)[..., None]
    return (result.reshape(rows_here, HEADS * HEAD_DIM).astype(jnp.bfloat16), arrived[:, None])


MESH = pl.DeviceIdType.MESH
SCALE = HEAD_DIM ** (-0.5)
REPEAT = HEADS // KV_HEADS
PLANE = KV_HEADS * HEAD_DIM
HOLDERS, GROUPS = 4, 8


def head_of(shape, axis):
    return (lax.broadcasted_iota(jnp.int32, shape, axis) * 3277) >> 18


def partner(index, flip):
    for bit in (1, 2, 4):
        if flip & bit:
            index = index + bit - 2 * bit * lax.rem(lax.div(index, bit), 2)
    return index


def split_dot(a, b):
    high = a.astype(jnp.bfloat16)
    low = (a - high.astype(jnp.float32)).astype(jnp.bfloat16)
    return jnp.dot(high, b, preferred_element_type=jnp.float32) + jnp.dot(
        low, b, preferred_element_type=jnp.float32
    )


def exact_dot(a, b):
    return jnp.dot(a, b, precision=lax.Precision.HIGHEST, preferred_element_type=jnp.float32)


def fused_kernel(
    tokens, gain, count, owners, targets, kept_rows, w_query, w_keyvalue, cache,
    attended, compacted,
    weight, pages, rows, leaving, projected, local, planes, fresh, sums, peaks,
    load_sem, keep_sem, row_send, row_recv, page_send, page_recv, proj_send, proj_recv,
    query_send, query_recv, fresh_send, fresh_recv, sum_send, sum_recv, peak_send, peak_recv,
):
    p = lax.axis_index("page")
    t = lax.axis_index("tensor")
    part = rows.shape[1]
    requests = part * HOLDERS
    slots = leaving.shape[0]
    keep = leaving.shape[1]
    cap = slots // HOLDERS
    page_rows = cache.shape[0] // slots

    loads = [
        pltpu.make_async_copy(cache, pages, load_sem.at[0]),
        pltpu.make_async_copy(w_query, weight.at[pl.ds(0, 320)], load_sem.at[1]),
        pltpu.make_async_copy(w_keyvalue, weight.at[pl.ds(320, 160)], load_sem.at[2]),
    ]
    for load in loads:
        load.start()

    barrier = pltpu.get_barrier_semaphore()
    for f in range(1, GROUPS):
        pl.semaphore_signal(barrier, inc=1, device_id=(p, partner(t, f)), device_id_type=MESH)
    for f in range(1, HOLDERS):
        pl.semaphore_signal(barrier, inc=1, device_id=(partner(p, f), t), device_id_type=MESH)

    weight[480:512] = jnp.zeros((32, weight.shape[1]), weight.dtype)
    gains = gain[...]
    gains = jnp.concatenate([gains[i : i + 1] for i in range(gains.shape[0])], axis=1)
    mine = tokens[p].astype(jnp.float32)
    square = jnp.mean(mine * mine, axis=-1, keepdims=True)
    rows[0] = (mine * lax.rsqrt(square + EPSILON) * gains).astype(jnp.bfloat16)
    pl.semaphore_wait(barrier, GROUPS + HOLDERS - 2)

    def pass_row(e, f):
        copy = pltpu.make_async_remote_copy(
            src_ref=rows.at[e],
            dst_ref=rows.at[e ^ f],
            send_sem=row_send.at[e ^ f],
            recv_sem=row_recv.at[e ^ f],
            device_id=(p, partner(t, f)),
            device_id_type=MESH,
        )
        copy.start()
        return copy

    moved = {4: pass_row(0, 4), 2: pass_row(0, 2), 1: pass_row(0, 1)}

    live = lax.broadcasted_iota(jnp.int32, (1, slots), 1) < count[...]
    target = jnp.where(live, targets[...], -1)
    owner_plus = owners[...].astype(jnp.float32) + 1.0

    def tags_of(shape, shift):
        at = lax.broadcasted_iota(jnp.int32, shape, 0) >> shift
        return jnp.sum(jnp.where(target == at, owner_plus, 0.0), axis=1, keepdims=True) - 1.0

    pairs = slots * KV_HEADS
    tags = tags_of((slots, slots), 0)
    tag_rows = tags_of((pairs, slots), 3)
    picks = jnp.concatenate([kept_rows[s] for s in range(slots)], axis=0).astype(jnp.float32)
    placed = (slots * keep, keep)
    repeat_rows = jnp.where(
        (lax.broadcasted_iota(jnp.int32, placed, 0) & (keep - 1))
        == lax.broadcasted_iota(jnp.int32, placed, 1),
        1.0,
        0.0,
    )
    code = lax.dot_general(
        repeat_rows.astype(jnp.bfloat16),
        picks.astype(jnp.bfloat16),
        (((1,), (1,)), ((), ())),
        preferred_element_type=jnp.float32,
    )
    at = lax.broadcasted_iota(jnp.int32, (slots * keep, slots), 0) >> 5
    code = jnp.where(target == at, code, -1.0)
    lane = lax.broadcasted_iota(jnp.int32, (slots * keep, page_rows), 1).astype(jnp.float32)
    choice = jnp.concatenate(
        [jnp.where(code[:, s : s + 1] == lane, 1.0, 0.0).astype(jnp.bfloat16) for s in range(slots)],
        axis=1,
    )
    loads[0].wait()
    out = jnp.dot(choice, pages[...], preferred_element_type=jnp.float32).astype(jnp.bfloat16)
    leaving[...] = out.reshape(leaving.shape)
    page_copies = []
    for f in range(1, HOLDERS):
        copy = pltpu.make_async_remote_copy(
            src_ref=leaving.at[pl.ds(partner(p, f) * cap, cap)],
            dst_ref=compacted.at[pl.ds(p * cap, cap)],
            send_sem=page_send.at[f],
            recv_sem=page_recv.at[f],
            device_id=(partner(p, f), t),
            device_id_type=MESH,
        )
        copy.start()
        page_copies.append(copy)
    kept = pltpu.make_async_copy(
        leaving.at[pl.ds(p * cap, cap)], compacted.at[pl.ds(p * cap, cap)], keep_sem
    )
    kept.start()

    moved[4].wait_recv()
    moved[6] = pass_row(4, 2)
    moved[5] = pass_row(4, 1)
    moved[2].wait_recv()
    moved[3] = pass_row(2, 1)
    loads[1].wait()
    loads[2].wait()
    moved[6].wait_recv()
    moved[7] = pass_row(6, 1)

    def project(first):
        batch = jnp.concatenate([rows[e] for e in range(first, GROUPS, 2)], axis=0)
        both = lax.dot_general(
            batch,
            weight[...],
            (((1,), (1,)), ((), ())),
            preferred_element_type=jnp.float32,
        ).astype(jnp.bfloat16)
        copies = []
        for n, e in enumerate(range(first, GROUPS, 2)):
            block = both[n * part : (n + 1) * part]
            if e == 0:
                local[t] = block
                continue
            projected[e] = block
            copy = pltpu.make_async_remote_copy(
                src_ref=projected.at[e],
                dst_ref=local.at[t],
                send_sem=proj_send.at[e],
                recv_sem=proj_recv.at[e],
                device_id=(p, partner(t, e)),
                device_id_type=MESH,
            )
            copy.start()
            copies.append(copy)
        return copies

    proj_copies = project(0)
    for e in (1, 3, 5, 7):
        moved[e].wait_recv()
    proj_copies += project(1)
    for copy in proj_copies:
        copy.wait_recv()

    blocks = [local[g].astype(jnp.float32) for g in range(GROUPS)]
    for k in range(REPEAT):
        planes[p, k] = jnp.concatenate(
            [b[:, k * HEAD_DIM : (k + 1) * HEAD_DIM] for b in blocks], axis=1
        ).astype(jnp.bfloat16)
    for n in range(2):
        fresh[p, n] = jnp.concatenate(
            [b[:, 320:480] for b in blocks[4 * n : 4 * n + 4]], axis=1
        ).astype(jnp.bfloat16)

    def to_holders(ref_of, send, recv):
        copies = []
        for f in range(1, HOLDERS):
            copy = pltpu.make_async_remote_copy(
                src_ref=ref_of(),
                dst_ref=ref_of(),
                send_sem=send.at[f],
                recv_sem=recv.at[f],
                device_id=(partner(p, f), t),
                device_id_type=MESH,
            )
            copy.start()
            copies.append(copy)
        return copies

    query_copies = to_holders(lambda: planes.at[p], query_send, query_recv)
    fresh_copies = to_holders(lambda: fresh.at[p], fresh_send, fresh_recv)

    def plane(ref, k):
        return jnp.concatenate([ref[h, k] for h in range(HOLDERS)], axis=0)

    member_row = jnp.where(
        tag_rows == lax.broadcasted_iota(jnp.int32, (pairs, requests), 1).astype(jnp.float32),
        1.0,
        0.0,
    ).astype(jnp.bfloat16)
    own_head = head_of((pairs, PLANE), 1) == (
        lax.broadcasted_iota(jnp.int32, (pairs, PLANE), 0) & (KV_HEADS - 1)
    )
    slot_rows = leaving[...].reshape(slots * keep, 2 * PLANE)
    for copy in query_copies:
        copy.wait_recv()

    spread = []
    for k in range(REPEAT):
        q = plane(planes, k)
        found = jnp.dot(member_row, q, preferred_element_type=jnp.float32)
        spread.append(jnp.where(own_head, found, 0.0).astype(jnp.bfloat16))
    scores = SCALE * lax.dot_general(
        jnp.concatenate(spread, axis=0),
        slot_rows[:, :PLANE],
        (((1,), (1,)), ((), ())),
        preferred_element_type=jnp.float32,
    )
    full = (REPEAT * pairs, slots * keep)
    same = ((lax.broadcasted_iota(jnp.int32, full, 0) >> 3) & (slots - 1)) == (
        lax.broadcasted_iota(jnp.int32, full, 1) >> 5
    )
    scores = jnp.where(same, scores, NEGATIVE)
    peak = jnp.max(scores, axis=1, keepdims=True)
    weights = jnp.where(same, jnp.exp(scores - peak), 0.0)
    total = jnp.sum(weights, axis=1, keepdims=True)
    mixed = jnp.dot(
        weights.astype(jnp.bfloat16), slot_rows[:, PLANE:], preferred_element_type=jnp.float32
    ) / total
    mixed = mixed.reshape(REPEAT, pairs, PLANE)
    mixed = jnp.where(own_head[None], mixed, 0.0)
    mixed = jnp.sum(mixed.reshape(REPEAT * slots, KV_HEADS, PLANE), axis=1)
    sums[p] = mixed.astype(jnp.bfloat16)
    lse = peak + jnp.log(total)
    wide = (REPEAT * pairs, 128)
    row_id = lax.broadcasted_iota(jnp.int32, wide, 0)
    at = (row_id >> 6) * KV_HEADS + (row_id & (KV_HEADS - 1))
    lse = jnp.where(lax.broadcasted_iota(jnp.int32, wide, 1) == at, lse, 0.0)
    lse = jnp.sum(lse.reshape(REPEAT, slots, KV_HEADS, 128), axis=2)
    lse = lse[0] + lse[1] + lse[2] + lse[3]
    peaks[p] = jnp.where(
        lax.broadcasted_iota(jnp.int32, (slots, 128), 1) == 127, tags, lse
    )
    peak_copies = to_holders(lambda: peaks.at[p], peak_send, peak_recv)
    sum_copies = to_holders(lambda: sums.at[p], sum_send, sum_recv)

    for copy in fresh_copies:
        copy.wait_recv()
    new_keys = plane(fresh, 0).astype(jnp.float32)
    new_values = plane(fresh, 1).astype(jnp.float32)
    own = jnp.zeros((requests, 128), jnp.float32)
    segment_head = head_of((PLANE, 128), 0)
    segment_lane = lax.broadcasted_iota(jnp.int32, (PLANE, 128), 1)
    for k in range(REPEAT):
        q = plane(planes, k).astype(jnp.float32)
        segment = jnp.where(segment_lane == segment_head + k * KV_HEADS, 1.0, 0.0)
        own += split_dot(q * new_keys, segment.astype(jnp.bfloat16))
    own = own * SCALE

    for copy in peak_copies:
        copy.wait_recv()
    every = HOLDERS * slots
    lse = peaks[...].reshape(every, 128)
    owner = lse[:, 127:128]
    where_slot = lax.broadcasted_iota(jnp.int32, (every, every), 0)
    where_lane = lax.broadcasted_iota(jnp.int32, (every, every), 1)
    owner_row = jnp.sum(jnp.where(where_slot == where_lane, owner, 0.0), axis=0, keepdims=True)
    request = lax.broadcasted_iota(jnp.int32, (requests, every), 0).astype(jnp.float32)
    member = jnp.where(request == owner_row, 1.0, 0.0)
    request = lax.broadcasted_iota(jnp.int32, (every, requests), 1).astype(jnp.float32)
    slot_member = jnp.where(request == owner, 1.0, 0.0)
    top = own
    for s in range(every):
        top = jnp.maximum(top, jnp.where(member[:, s : s + 1] > 0.0, lse[s : s + 1], NEGATIVE))
    factor = jnp.exp(lse - exact_dot(slot_member, top))
    factor = jnp.where(owner >= 0.0, factor, 0.0)
    own_weight = jnp.exp(own - top)
    whole = exact_dot(member, factor) + own_weight
    slot_whole = exact_dot(slot_member, whole)
    slot_part = factor / jnp.where(owner >= 0.0, slot_whole, 1.0)
    own_part = own_weight / whole
    parts = jnp.concatenate([slot_part, own_part], axis=0)

    for copy in sum_copies:
        copy.wait_recv()
    slot_sums = sums[...].astype(jnp.float32).reshape(HOLDERS, REPEAT, slots, PLANE)
    member = member.astype(jnp.bfloat16)
    spread_head = head_of((128, PLANE), 1)
    spread_row = lax.broadcasted_iota(jnp.int32, (128, PLANE), 0)
    results = []
    for k in range(REPEAT):
        expand = jnp.where(spread_row == spread_head + k * KV_HEADS, 1.0, 0.0)
        shares = split_dot(parts, expand.astype(jnp.bfloat16))
        weighted = (shares[:every] * slot_sums[:, k].reshape(every, PLANE)).astype(jnp.bfloat16)
        results.append(
            jnp.dot(member, weighted, preferred_element_type=jnp.float32)
            + shares[every:] * new_values
        )
    attended[...] = jnp.concatenate(
        [
            results[k][:, g * HEAD_DIM : (g + 1) * HEAD_DIM]
            for g in range(KV_HEADS)
            for k in range(REPEAT)
        ],
        axis=1,
    ).astype(jnp.bfloat16)

    for copy in page_copies:
        copy.wait_recv()
    kept.wait()
    for copy in (
        list(moved.values()) + page_copies + proj_copies + query_copies + fresh_copies
        + peak_copies + sum_copies
    ):
        copy.wait_send()


def fused_device(
    tokens, norm_gain, w_query, w_keyvalue, cache, page_count, page_owner, keep_rows, dest_slot
):
    slots, _, page_rows, width = cache.shape
    keep = keep_rows.shape[2]
    requests, model = tokens.shape
    part = requests // HOLDERS
    vmem = pl.BlockSpec(memory_space=pltpu.VMEM)
    anywhere = pl.BlockSpec(memory_space=pl.ANY)
    bf16, f32 = jnp.bfloat16, jnp.float32
    dma = pltpu.SemaphoreType.DMA
    attended, compacted = pl.pallas_call(
        fused_kernel,
        out_shape=(
            jax.ShapeDtypeStruct((requests, HEADS * HEAD_DIM), bf16),
            jax.ShapeDtypeStruct((slots, keep, width), bf16),
        ),
        in_specs=[vmem] * 6 + [anywhere] * 3,
        out_specs=(vmem, anywhere),
        scratch_shapes=[
            pltpu.VMEM((512, model), bf16),
            pltpu.VMEM((slots * page_rows, width), bf16),
            pltpu.VMEM((GROUPS, part, model), bf16),
            pltpu.VMEM((slots, keep, width), bf16),
            pltpu.VMEM((GROUPS, part, 512), bf16),
            pltpu.VMEM((GROUPS, part, 512), bf16),
            pltpu.VMEM((HOLDERS, REPEAT, part, PLANE), bf16),
            pltpu.VMEM((HOLDERS, 2, part, PLANE), bf16),
            pltpu.VMEM((HOLDERS, REPEAT * slots, PLANE), bf16),
            pltpu.VMEM((HOLDERS, slots, 128), f32),
            dma((3,)),
            dma,
            dma((GROUPS,)),
            dma((GROUPS,)),
            dma((HOLDERS,)),
            dma((HOLDERS,)),
            dma((GROUPS,)),
            dma((GROUPS,)),
        ]
        + [dma((HOLDERS,))] * 8,
        compiler_params=pltpu.CompilerParams(
            collective_id=0, has_side_effects=True, vmem_limit_bytes=48 * 1024 * 1024
        ),
        cost_estimate=pl.CostEstimate(
            flops=1_500_000_000, bytes_accessed=7_000_000, transcendentals=70_000
        ),
    )(
        tokens.reshape(HOLDERS, part, model),
        norm_gain.reshape(model // 128, 128),
        page_count,
        page_owner.reshape(1, slots),
        dest_slot.reshape(1, slots),
        keep_rows,
        w_query.T,
        w_keyvalue.T,
        cache.reshape(slots * page_rows, width),
    )
    return attended, compacted[:, None]


def local_step(sizes, tokens, norm_gain, w_query, w_keyvalue, cache, *rest):
    fits = (
        sizes == {"page": HOLDERS, "tensor": GROUPS}
        and tokens.shape[0] == 64
        and cache.shape[0] == 8
        and rest[2].shape[2] == 32
    )
    step = fused_device if fits else per_device
    return step(tokens, norm_gain, w_query, w_keyvalue, cache, *rest)


def solution(mesh):
    return jax.shard_map(
        functools.partial(local_step, dict(mesh.shape)),
        mesh=mesh,
        in_specs=(
            P("tensor", None),
            P(),
            P(None, "tensor"),
            P(None, "tensor"),
            P("page", "tensor", None, None),
            P("page", "tensor"),
            P("page", "tensor"),
            P("page", "tensor", None),
            P("page", "tensor"),
        ),
        out_specs=(P("tensor", None), P("page", "tensor", None, None)),
        check_vma=False,
    )
```

```python
import functools

import jax
import jax.numpy as jnp
from jax import lax
from jax.experimental import pallas as pl
from jax.experimental.pallas import tpu as pltpu
from jax.sharding import PartitionSpec as P

HEADS = 32
KV_HEADS = 8
HEAD_DIM = 80


EPSILON = 1e-05
NEGATIVE = -1e30


def per_device(
    tokens, norm_gain, w_query, w_keyvalue, cache, page_count, page_owner, keep_rows, dest_slot
):
    holders = lax.axis_size("page")
    groups = lax.axis_size("tensor")
    rows_here = tokens.shape[0]
    sources = cache.shape[0]
    keep_count = keep_rows.shape[2]
    row_width = cache.shape[3]
    capacity = (sources + holders - 1) // holders
    targets = capacity * holders
    repeat_count = HEADS // KV_HEADS
    score_scale = HEAD_DIM ** (-0.5)
    widened = tokens.astype(jnp.float32)
    normed = (
        widened
        * lax.rsqrt(jnp.mean(widened * widened, axis=-1, keepdims=True) + EPSILON)
        * norm_gain
    ).astype(jnp.bfloat16)
    portion = lax.all_gather(normed, "tensor", axis=0, tiled=True)
    query_part = jnp.dot(portion, w_query, preferred_element_type=jnp.float32)
    pair_part = jnp.dot(portion, w_keyvalue, preferred_element_type=jnp.float32)
    projected = jnp.concatenate([query_part, pair_part], axis=1).astype(jnp.bfloat16)
    local_heads = lax.all_to_all(
        projected, "tensor", split_axis=0, concat_axis=1, tiled=True
    ).reshape(rows_here, groups, -1)
    query_cols = w_query.shape[1]
    queries = local_heads[:, :, :query_cols].reshape(rows_here, KV_HEADS, repeat_count, HEAD_DIM)
    fresh_kv = local_heads[:, :, query_cols:].reshape(rows_here, 2, KV_HEADS, HEAD_DIM)
    new_keys = fresh_kv[:, 0]
    new_values = fresh_kv[:, 1]
    retained = jax.vmap(lambda one_page, row_picks: one_page[row_picks])(
        cache[:, 0], keep_rows[:, 0]
    )
    is_live = jnp.arange(sources) < page_count[0, 0]
    owners = page_owner[:, 0]
    chosen = (dest_slot[:, 0][None, :] == jnp.arange(targets)[:, None]) & is_live[None, :]
    outgoing = jnp.einsum(
        "ts,sjc->tjc", chosen.astype(jnp.bfloat16), retained, preferred_element_type=jnp.float32
    ).astype(jnp.bfloat16)
    out_tags = jnp.sum(jnp.where(chosen, owners[None, :] + 1, 0), axis=1) - 1
    arrived, arrived_tags = (
        lax.all_to_all(
            outgoing.reshape(holders, capacity, keep_count, row_width),
            "page",
            split_axis=0,
            concat_axis=0,
            tiled=True,
        ),
        lax.all_to_all(
            out_tags.reshape(holders, capacity), "page", split_axis=0, concat_axis=0, tiled=True
        ),
    )
    arrived = arrived.reshape(targets, keep_count, row_width)
    arrived_tags = arrived_tags.reshape(targets)
    slot_count = arrived.shape[0]
    active = arrived_tags >= 0
    owner_idx = jnp.maximum(arrived_tags, 0)
    picked = jnp.take(queries, owner_idx, axis=0)
    slot_keys = arrived[:, :, : KV_HEADS * HEAD_DIM].reshape(
        slot_count, keep_count, KV_HEADS, HEAD_DIM
    )
    slot_values = arrived[:, :, KV_HEADS * HEAD_DIM :].reshape(
        slot_count, keep_count, KV_HEADS, HEAD_DIM
    )
    scores = (
        jnp.einsum("sgkd,sjgd->sgkj", picked, slot_keys, preferred_element_type=jnp.float32)
        * score_scale
    )
    member = (owner_idx[None, :] == jnp.arange(rows_here)[:, None]) & active[None, :]
    slot_peak = jnp.max(scores, axis=3)
    local_peak = jnp.max(jnp.where(member[:, :, None, None], slot_peak[None], NEGATIVE), axis=1)
    own_score = (
        jnp.einsum("rgkd,rgd->rgk", queries, new_keys, preferred_element_type=jnp.float32)
        * score_scale
    )
    row_peak = jnp.maximum(lax.pmax(local_peak, "page"), own_score)
    shifted = scores - jnp.take(row_peak, owner_idx, axis=0)[..., None]
    weights = jnp.where(active[:, None, None, None], jnp.exp(shifted), 0.0)
    slot_total = jnp.sum(weights, axis=3)
    slot_out = jnp.einsum(
        "sgkj,sjgd->sgkd",
        weights.astype(jnp.bfloat16),
        slot_values,
        preferred_element_type=jnp.float32,
    )
    member_weight = member.astype(jnp.float32)
    part_total = jnp.einsum(
        "rs,sgk->rgk", member_weight, slot_total, precision=lax.Precision.HIGHEST
    )
    part_out = jnp.einsum("rs,sgkd->rgkd", member_weight, slot_out, precision=lax.Precision.HIGHEST)
    sum_out, sum_total = lax.psum((part_out, part_total), "page")
    own_weight = jnp.exp(own_score - row_peak)
    mixed = sum_out + own_weight[..., None] * new_values[:, :, None, :].astype(jnp.float32)
    result = mixed / (sum_total + own_weight)[..., None]
    return (result.reshape(rows_here, HEADS * HEAD_DIM).astype(jnp.bfloat16), arrived[:, None])


MESH = pl.DeviceIdType.MESH
SCALE = HEAD_DIM ** (-0.5)
REPEAT = HEADS // KV_HEADS
PLANE = KV_HEADS * HEAD_DIM
HOLDERS, GROUPS = 4, 8


def head_of(shape, axis):
    return (lax.broadcasted_iota(jnp.int32, shape, axis) * 3277) >> 18


def partner(index, flip):
    for bit in (1, 2, 4):
        if flip & bit:
            index = index + bit - 2 * bit * lax.rem(lax.div(index, bit), 2)
    return index


def split_dot(a, b):
    high = a.astype(jnp.bfloat16)
    low = (a - high.astype(jnp.float32)).astype(jnp.bfloat16)
    return jnp.dot(high, b, preferred_element_type=jnp.float32) + jnp.dot(
        low, b, preferred_element_type=jnp.float32
    )


def exact_dot(a, b):
    return jnp.dot(a, b, precision=lax.Precision.HIGHEST, preferred_element_type=jnp.float32)


def fused_kernel(
    tokens_in, gain_in, count_in, owners_in, targets_in, kept_in, w_query, w_keyvalue, cache,
    attended, compacted,
    tokens, gain, count, owners, targets, kept_rows, weight, pages, rows, leaving, projected, local, planes, fresh, sums, peaks,
    load_sem, keep_sem, row_send, row_recv, page_send, page_recv, proj_send, proj_recv,
    query_send, query_recv, fresh_send, fresh_recv, sum_send, sum_recv, peak_send, peak_recv,
):
    p = lax.axis_index("page")
    t = lax.axis_index("tensor")
    part = rows.shape[2]
    requests = part * HOLDERS
    slots = leaving.shape[0]
    keep = leaving.shape[1]
    cap = slots // HOLDERS
    page_rows = cache.shape[0] // slots

    loads = [
        pltpu.make_async_copy(tokens_in.at[p], tokens, load_sem.at[3]),
        pltpu.make_async_copy(gain_in, gain, load_sem.at[4]),
        pltpu.make_async_copy(count_in, count, load_sem.at[5]),
        pltpu.make_async_copy(owners_in, owners, load_sem.at[6]),
        pltpu.make_async_copy(targets_in, targets, load_sem.at[7]),
        pltpu.make_async_copy(kept_in, kept_rows, load_sem.at[8]),
        pltpu.make_async_copy(cache, pages, load_sem.at[0]),
        pltpu.make_async_copy(w_query, weight.at[pl.ds(0, 320)], load_sem.at[1]),
        pltpu.make_async_copy(w_keyvalue, weight.at[pl.ds(320, 160)], load_sem.at[2]),
    ]
    for load in loads:
        load.start()

    barrier = pltpu.get_barrier_semaphore()
    for f in range(1, GROUPS):
        pl.semaphore_signal(barrier, inc=1, device_id=(p, partner(t, f)), device_id_type=MESH)
    for f in range(1, HOLDERS):
        pl.semaphore_signal(barrier, inc=1, device_id=(partner(p, f), t), device_id_type=MESH)

    weight[480:512] = jnp.zeros((32, weight.shape[1]), weight.dtype)
    loads[0].wait()
    loads[1].wait()
    gains = gain[...]
    gains = jnp.concatenate([gains[i : i + 1] for i in range(gains.shape[0])], axis=1)
    mine = tokens[...].astype(jnp.float32)
    square = jnp.mean(mine * mine, axis=-1, keepdims=True)
    normed = (mine * lax.rsqrt(square + EPSILON) * gains).astype(jnp.bfloat16)
    half = normed.shape[1] // 2
    rows[0, 0] = normed[:, :half]
    rows[1, 0] = normed[:, half:]
    pl.semaphore_wait(barrier, GROUPS + HOLDERS - 2)

    def pass_row(h, e, f):
        copy = pltpu.make_async_remote_copy(
            src_ref=rows.at[h, e],
            dst_ref=rows.at[h, e ^ f],
            send_sem=row_send.at[h, e ^ f],
            recv_sem=row_recv.at[h, e ^ f],
            device_id=(p, partner(t, f)),
            device_id_type=MESH,
        )
        copy.start()
        return copy

    moved = {}
    for h in range(2):
        for f in (4, 2, 1):
            moved[h, f] = pass_row(h, 0, f)

    def forward(h, e):
        moved[h, e].wait_recv()
        if e == 4:
            moved[h, 6] = pass_row(h, 4, 2)
        moved[h, e + 1] = pass_row(h, e, 1)

    for load in loads[2:6]:
        load.wait()
    live = lax.broadcasted_iota(jnp.int32, (1, slots), 1) < count[...]
    target = jnp.where(live, targets[...], -1)
    owner_plus = owners[...].astype(jnp.float32) + 1.0

    def tags_of(shape, shift):
        at = lax.broadcasted_iota(jnp.int32, shape, 0) >> shift
        return jnp.sum(jnp.where(target == at, owner_plus, 0.0), axis=1, keepdims=True) - 1.0

    pairs = slots * KV_HEADS
    tags = tags_of((slots, slots), 0)
    tag_rows = tags_of((pairs, slots), 3)
    picks = jnp.concatenate([kept_rows[s] for s in range(slots)], axis=0).astype(jnp.float32)
    placed = (slots * keep, keep)
    repeat_rows = jnp.where(
        (lax.broadcasted_iota(jnp.int32, placed, 0) & (keep - 1))
        == lax.broadcasted_iota(jnp.int32, placed, 1),
        1.0,
        0.0,
    )
    code = lax.dot_general(
        repeat_rows.astype(jnp.bfloat16),
        picks.astype(jnp.bfloat16),
        (((1,), (1,)), ((), ())),
        preferred_element_type=jnp.float32,
    )
    at = lax.broadcasted_iota(jnp.int32, (slots * keep, slots), 0) >> 5
    code = jnp.where(target == at, code, -1.0)
    lane = lax.broadcasted_iota(jnp.int32, (slots * keep, page_rows), 1).astype(jnp.float32)
    choice = jnp.concatenate(
        [jnp.where(code[:, s : s + 1] == lane, 1.0, 0.0).astype(jnp.bfloat16) for s in range(slots)],
        axis=1,
    )
    loads[6].wait()
    forward(0, 4)
    forward(0, 2)
    left = jnp.dot(choice, pages[:, :PLANE], preferred_element_type=jnp.float32)
    forward(1, 4)
    forward(1, 2)
    right = jnp.dot(choice, pages[:, PLANE:], preferred_element_type=jnp.float32)
    out = jnp.concatenate([left, right], axis=1).astype(jnp.bfloat16)
    leaving[...] = out.reshape(leaving.shape)
    page_copies = []
    for f in range(1, HOLDERS):
        copy = pltpu.make_async_remote_copy(
            src_ref=leaving.at[pl.ds(partner(p, f) * cap, cap)],
            dst_ref=compacted.at[pl.ds(p * cap, cap)],
            send_sem=page_send.at[f],
            recv_sem=page_recv.at[f],
            device_id=(partner(p, f), t),
            device_id_type=MESH,
        )
        copy.start()
        page_copies.append(copy)
    kept = pltpu.make_async_copy(
        leaving.at[pl.ds(p * cap, cap)], compacted.at[pl.ds(p * cap, cap)], keep_sem
    )
    kept.start()

    loads[7].wait()
    loads[8].wait()
    forward(0, 6)
    forward(1, 6)

    def project(first):
        both = 0.0
        for h in range(2):
            if first == 1:
                for e in (1, 3, 5, 7):
                    moved[h, e].wait_recv()
            both += lax.dot_general(
                jnp.concatenate([rows[h, e] for e in range(first, GROUPS, 2)], axis=0),
                weight[:, h * half : (h + 1) * half],
                (((1,), (1,)), ((), ())),
                preferred_element_type=jnp.float32,
            )
        both = both.astype(jnp.bfloat16)
        copies = []
        for n, e in enumerate(range(first, GROUPS, 2)):
            block = both[n * part : (n + 1) * part]
            if e == 0:
                local[t] = block
                continue
            projected[e] = block
            copy = pltpu.make_async_remote_copy(
                src_ref=projected.at[e],
                dst_ref=local.at[t],
                send_sem=proj_send.at[e],
                recv_sem=proj_recv.at[e],
                device_id=(p, partner(t, e)),
                device_id_type=MESH,
            )
            copy.start()
            copies.append(copy)
        return copies

    proj_copies = project(0)
    proj_copies += project(1)
    for copy in proj_copies:
        copy.wait_recv()

    blocks = [local[g].astype(jnp.float32) for g in range(GROUPS)]
    for k in range(REPEAT):
        planes[p, k] = jnp.concatenate(
            [b[:, k * HEAD_DIM : (k + 1) * HEAD_DIM] for b in blocks], axis=1
        ).astype(jnp.bfloat16)
    for n in range(2):
        fresh[p, n] = jnp.concatenate(
            [b[:, 320:480] for b in blocks[4 * n : 4 * n + 4]], axis=1
        ).astype(jnp.bfloat16)

    def to_holders(ref_of, send, recv):
        copies = []
        for f in range(1, HOLDERS):
            copy = pltpu.make_async_remote_copy(
                src_ref=ref_of(),
                dst_ref=ref_of(),
                send_sem=send.at[f],
                recv_sem=recv.at[f],
                device_id=(partner(p, f), t),
                device_id_type=MESH,
            )
            copy.start()
            copies.append(copy)
        return copies

    query_copies = to_holders(lambda: planes.at[p], query_send, query_recv)
    fresh_copies = to_holders(lambda: fresh.at[p], fresh_send, fresh_recv)

    def plane(ref, k):
        return jnp.concatenate([ref[h, k] for h in range(HOLDERS)], axis=0)

    member_row = jnp.where(
        tag_rows == lax.broadcasted_iota(jnp.int32, (pairs, requests), 1).astype(jnp.float32),
        1.0,
        0.0,
    ).astype(jnp.bfloat16)
    own_head = head_of((pairs, PLANE), 1) == (
        lax.broadcasted_iota(jnp.int32, (pairs, PLANE), 0) & (KV_HEADS - 1)
    )
    slot_rows = leaving[...].reshape(slots * keep, 2 * PLANE)
    for copy in query_copies:
        copy.wait_recv()

    spread = []
    for k in range(REPEAT):
        q = plane(planes, k)
        found = jnp.dot(member_row, q, preferred_element_type=jnp.float32)
        spread.append(jnp.where(own_head, found, 0.0).astype(jnp.bfloat16))
    scores = SCALE * lax.dot_general(
        jnp.concatenate(spread, axis=0),
        slot_rows[:, :PLANE],
        (((1,), (1,)), ((), ())),
        preferred_element_type=jnp.float32,
    )
    full = (REPEAT * pairs, slots * keep)
    same = ((lax.broadcasted_iota(jnp.int32, full, 0) >> 3) & (slots - 1)) == (
        lax.broadcasted_iota(jnp.int32, full, 1) >> 5
    )
    scores = jnp.where(same, scores, NEGATIVE)
    peak = jnp.max(scores, axis=1, keepdims=True)
    weights = jnp.where(same, jnp.exp(scores - peak), 0.0)
    total = jnp.sum(weights, axis=1, keepdims=True)
    mixed = jnp.dot(
        weights.astype(jnp.bfloat16), slot_rows[:, PLANE:], preferred_element_type=jnp.float32
    ) / total
    mixed = mixed.reshape(REPEAT, pairs, PLANE)
    mixed = jnp.where(own_head[None], mixed, 0.0)
    mixed = jnp.sum(mixed.reshape(REPEAT * slots, KV_HEADS, PLANE), axis=1)
    sums[p] = mixed.astype(jnp.bfloat16)
    lse = peak + jnp.log(total)
    wide = (REPEAT * pairs, 128)
    row_id = lax.broadcasted_iota(jnp.int32, wide, 0)
    at = (row_id >> 6) * KV_HEADS + (row_id & (KV_HEADS - 1))
    lse = jnp.where(lax.broadcasted_iota(jnp.int32, wide, 1) == at, lse, 0.0)
    lse = jnp.sum(lse.reshape(REPEAT, slots, KV_HEADS, 128), axis=2)
    lse = lse[0] + lse[1] + lse[2] + lse[3]
    peaks[p] = jnp.where(
        lax.broadcasted_iota(jnp.int32, (slots, 128), 1) == 127, tags, lse
    )
    peak_copies = to_holders(lambda: peaks.at[p], peak_send, peak_recv)
    sum_copies = to_holders(lambda: sums.at[p], sum_send, sum_recv)

    for copy in fresh_copies:
        copy.wait_recv()
    new_keys = plane(fresh, 0).astype(jnp.float32)
    new_values = plane(fresh, 1).astype(jnp.float32)
    own = jnp.zeros((requests, 128), jnp.float32)
    segment_head = head_of((PLANE, 128), 0)
    segment_lane = lax.broadcasted_iota(jnp.int32, (PLANE, 128), 1)
    for k in range(REPEAT):
        q = plane(planes, k).astype(jnp.float32)
        segment = jnp.where(segment_lane == segment_head + k * KV_HEADS, 1.0, 0.0)
        own += split_dot(q * new_keys, segment.astype(jnp.bfloat16))
    own = own * SCALE

    for copy in peak_copies:
        copy.wait_recv()
    every = HOLDERS * slots
    lse = peaks[...].reshape(every, 128)
    owner = lse[:, 127:128]
    where_slot = lax.broadcasted_iota(jnp.int32, (every, every), 0)
    where_lane = lax.broadcasted_iota(jnp.int32, (every, every), 1)
    owner_row = jnp.sum(jnp.where(where_slot == where_lane, owner, 0.0), axis=0, keepdims=True)
    request = lax.broadcasted_iota(jnp.int32, (requests, every), 0).astype(jnp.float32)
    member = jnp.where(request == owner_row, 1.0, 0.0)
    request = lax.broadcasted_iota(jnp.int32, (every, requests), 1).astype(jnp.float32)
    slot_member = jnp.where(request == owner, 1.0, 0.0)
    top = own
    for s in range(every):
        top = jnp.maximum(top, jnp.where(member[:, s : s + 1] > 0.0, lse[s : s + 1], NEGATIVE))
    factor = jnp.exp(lse - exact_dot(slot_member, top))
    factor = jnp.where(owner >= 0.0, factor, 0.0)
    own_weight = jnp.exp(own - top)
    whole = exact_dot(member, factor) + own_weight
    slot_whole = exact_dot(slot_member, whole)
    slot_part = factor / jnp.where(owner >= 0.0, slot_whole, 1.0)
    own_part = own_weight / whole
    parts = jnp.concatenate([slot_part, own_part], axis=0)

    for copy in sum_copies:
        copy.wait_recv()
    slot_sums = sums[...].astype(jnp.float32).reshape(HOLDERS, REPEAT, slots, PLANE)
    member = member.astype(jnp.bfloat16)
    spread_head = head_of((128, PLANE), 1)
    spread_row = lax.broadcasted_iota(jnp.int32, (128, PLANE), 0)
    results = []
    for k in range(REPEAT):
        expand = jnp.where(spread_row == spread_head + k * KV_HEADS, 1.0, 0.0)
        shares = split_dot(parts, expand.astype(jnp.bfloat16))
        weighted = (shares[:every] * slot_sums[:, k].reshape(every, PLANE)).astype(jnp.bfloat16)
        results.append(
            jnp.dot(member, weighted, preferred_element_type=jnp.float32)
            + shares[every:] * new_values
        )
    attended[...] = jnp.concatenate(
        [
            results[k][:, g * HEAD_DIM : (g + 1) * HEAD_DIM]
            for g in range(KV_HEADS)
            for k in range(REPEAT)
        ],
        axis=1,
    ).astype(jnp.bfloat16)

    for copy in page_copies:
        copy.wait_recv()
    kept.wait()
    for copy in (
        list(moved.values()) + page_copies + proj_copies + query_copies + fresh_copies
        + peak_copies + sum_copies
    ):
        copy.wait_send()


def fused_device(
    tokens, norm_gain, w_query, w_keyvalue, cache, page_count, page_owner, keep_rows, dest_slot
):
    slots, _, page_rows, width = cache.shape
    keep = keep_rows.shape[2]
    requests, model = tokens.shape
    part = requests // HOLDERS
    vmem = pl.BlockSpec(memory_space=pltpu.VMEM)
    anywhere = pl.BlockSpec(memory_space=pl.ANY)
    bf16, f32 = jnp.bfloat16, jnp.float32
    dma = pltpu.SemaphoreType.DMA
    attended, compacted = pl.pallas_call(
        fused_kernel,
        out_shape=(
            jax.ShapeDtypeStruct((requests, HEADS * HEAD_DIM), bf16),
            jax.ShapeDtypeStruct((slots, keep, width), bf16),
        ),
        in_specs=[anywhere] * 9,
        out_specs=(vmem, anywhere),
        scratch_shapes=[
            pltpu.VMEM((part, model), bf16),
            pltpu.VMEM((model // 128, 128), f32),
            pltpu.VMEM((1, 1), jnp.int32),
            pltpu.VMEM((1, slots), jnp.int32),
            pltpu.VMEM((1, slots), jnp.int32),
            pltpu.VMEM(keep_rows.shape, jnp.int32),
            pltpu.VMEM((512, model), bf16),
            pltpu.VMEM((slots * page_rows, width), bf16),
            pltpu.VMEM((2, GROUPS, part, model // 2), bf16),
            pltpu.VMEM((slots, keep, width), bf16),
            pltpu.VMEM((GROUPS, part, 512), bf16),
            pltpu.VMEM((GROUPS, part, 512), bf16),
            pltpu.VMEM((HOLDERS, REPEAT, part, PLANE), bf16),
            pltpu.VMEM((HOLDERS, 2, part, PLANE), bf16),
            pltpu.VMEM((HOLDERS, REPEAT * slots, PLANE), bf16),
            pltpu.VMEM((HOLDERS, slots, 128), f32),
            dma((9,)),
            dma,
            dma((2, GROUPS)),
            dma((2, GROUPS)),
            dma((HOLDERS,)),
            dma((HOLDERS,)),
            dma((GROUPS,)),
            dma((GROUPS,)),
        ]
        + [dma((HOLDERS,))] * 8,
        compiler_params=pltpu.CompilerParams(
            collective_id=0, has_side_effects=True, vmem_limit_bytes=60 * 1024 * 1024
        ),
        cost_estimate=pl.CostEstimate(
            flops=1_500_000_000, bytes_accessed=7_000_000, transcendentals=70_000
        ),
    )(
        tokens.reshape(HOLDERS, part, model),
        norm_gain.reshape(model // 128, 128),
        page_count,
        page_owner.reshape(1, slots),
        dest_slot.reshape(1, slots),
        keep_rows,
        w_query.T,
        w_keyvalue.T,
        cache.reshape(slots * page_rows, width),
    )
    return attended, compacted[:, None]


def local_step(sizes, tokens, norm_gain, w_query, w_keyvalue, cache, *rest):
    fits = (
        sizes == {"page": HOLDERS, "tensor": GROUPS}
        and tokens.shape[0] == 64
        and cache.shape[0] == 8
        and rest[2].shape[2] == 32
    )
    step = fused_device if fits else per_device
    return step(tokens, norm_gain, w_query, w_keyvalue, cache, *rest)


def solution(mesh):
    return jax.shard_map(
        functools.partial(local_step, dict(mesh.shape)),
        mesh=mesh,
        in_specs=(
            P("tensor", None),
            P(),
            P(None, "tensor"),
            P(None, "tensor"),
            P("page", "tensor", None, None),
            P("page", "tensor"),
            P("page", "tensor"),
            P("page", "tensor", None),
            P("page", "tensor"),
        ),
        out_specs=(P("tensor", None), P("page", "tensor", None, None)),
        check_vma=False,
    )
```

```python
import functools

import jax
import jax.numpy as jnp
from jax import lax
from jax.experimental import pallas as pl
from jax.experimental.pallas import tpu as pltpu
from jax.sharding import PartitionSpec as P

HEADS = 32
KV_HEADS = 8
HEAD_DIM = 80


EPSILON = 1e-05
NEGATIVE = -1e30


def per_device(
    tokens, norm_gain, w_query, w_keyvalue, cache, page_count, page_owner, keep_rows, dest_slot
):
    holders = lax.axis_size("page")
    groups = lax.axis_size("tensor")
    rows_here = tokens.shape[0]
    sources = cache.shape[0]
    keep_count = keep_rows.shape[2]
    row_width = cache.shape[3]
    capacity = (sources + holders - 1) // holders
    targets = capacity * holders
    repeat_count = HEADS // KV_HEADS
    score_scale = HEAD_DIM ** (-0.5)
    widened = tokens.astype(jnp.float32)
    normed = (
        widened
        * lax.rsqrt(jnp.mean(widened * widened, axis=-1, keepdims=True) + EPSILON)
        * norm_gain
    ).astype(jnp.bfloat16)
    portion = lax.all_gather(normed, "tensor", axis=0, tiled=True)
    query_part = jnp.dot(portion, w_query, preferred_element_type=jnp.float32)
    pair_part = jnp.dot(portion, w_keyvalue, preferred_element_type=jnp.float32)
    projected = jnp.concatenate([query_part, pair_part], axis=1).astype(jnp.bfloat16)
    local_heads = lax.all_to_all(
        projected, "tensor", split_axis=0, concat_axis=1, tiled=True
    ).reshape(rows_here, groups, -1)
    query_cols = w_query.shape[1]
    queries = local_heads[:, :, :query_cols].reshape(rows_here, KV_HEADS, repeat_count, HEAD_DIM)
    fresh_kv = local_heads[:, :, query_cols:].reshape(rows_here, 2, KV_HEADS, HEAD_DIM)
    new_keys = fresh_kv[:, 0]
    new_values = fresh_kv[:, 1]
    retained = jax.vmap(lambda one_page, row_picks: one_page[row_picks])(
        cache[:, 0], keep_rows[:, 0]
    )
    is_live = jnp.arange(sources) < page_count[0, 0]
    owners = page_owner[:, 0]
    chosen = (dest_slot[:, 0][None, :] == jnp.arange(targets)[:, None]) & is_live[None, :]
    outgoing = jnp.einsum(
        "ts,sjc->tjc", chosen.astype(jnp.bfloat16), retained, preferred_element_type=jnp.float32
    ).astype(jnp.bfloat16)
    out_tags = jnp.sum(jnp.where(chosen, owners[None, :] + 1, 0), axis=1) - 1
    arrived, arrived_tags = (
        lax.all_to_all(
            outgoing.reshape(holders, capacity, keep_count, row_width),
            "page",
            split_axis=0,
            concat_axis=0,
            tiled=True,
        ),
        lax.all_to_all(
            out_tags.reshape(holders, capacity), "page", split_axis=0, concat_axis=0, tiled=True
        ),
    )
    arrived = arrived.reshape(targets, keep_count, row_width)
    arrived_tags = arrived_tags.reshape(targets)
    slot_count = arrived.shape[0]
    active = arrived_tags >= 0
    owner_idx = jnp.maximum(arrived_tags, 0)
    picked = jnp.take(queries, owner_idx, axis=0)
    slot_keys = arrived[:, :, : KV_HEADS * HEAD_DIM].reshape(
        slot_count, keep_count, KV_HEADS, HEAD_DIM
    )
    slot_values = arrived[:, :, KV_HEADS * HEAD_DIM :].reshape(
        slot_count, keep_count, KV_HEADS, HEAD_DIM
    )
    scores = (
        jnp.einsum("sgkd,sjgd->sgkj", picked, slot_keys, preferred_element_type=jnp.float32)
        * score_scale
    )
    member = (owner_idx[None, :] == jnp.arange(rows_here)[:, None]) & active[None, :]
    slot_peak = jnp.max(scores, axis=3)
    local_peak = jnp.max(jnp.where(member[:, :, None, None], slot_peak[None], NEGATIVE), axis=1)
    own_score = (
        jnp.einsum("rgkd,rgd->rgk", queries, new_keys, preferred_element_type=jnp.float32)
        * score_scale
    )
    row_peak = jnp.maximum(lax.pmax(local_peak, "page"), own_score)
    shifted = scores - jnp.take(row_peak, owner_idx, axis=0)[..., None]
    weights = jnp.where(active[:, None, None, None], jnp.exp(shifted), 0.0)
    slot_total = jnp.sum(weights, axis=3)
    slot_out = jnp.einsum(
        "sgkj,sjgd->sgkd",
        weights.astype(jnp.bfloat16),
        slot_values,
        preferred_element_type=jnp.float32,
    )
    member_weight = member.astype(jnp.float32)
    part_total = jnp.einsum(
        "rs,sgk->rgk", member_weight, slot_total, precision=lax.Precision.HIGHEST
    )
    part_out = jnp.einsum("rs,sgkd->rgkd", member_weight, slot_out, precision=lax.Precision.HIGHEST)
    sum_out, sum_total = lax.psum((part_out, part_total), "page")
    own_weight = jnp.exp(own_score - row_peak)
    mixed = sum_out + own_weight[..., None] * new_values[:, :, None, :].astype(jnp.float32)
    result = mixed / (sum_total + own_weight)[..., None]
    return (result.reshape(rows_here, HEADS * HEAD_DIM).astype(jnp.bfloat16), arrived[:, None])


MESH = pl.DeviceIdType.MESH
SCALE = HEAD_DIM ** (-0.5)
REPEAT = HEADS // KV_HEADS
PLANE = KV_HEADS * HEAD_DIM
HOLDERS, GROUPS = 4, 8


def head_of(shape, axis):
    return (lax.broadcasted_iota(jnp.int32, shape, axis) * 3277) >> 18


def partner(index, flip):
    for bit in (1, 2, 4):
        if flip & bit:
            index = index + bit - 2 * bit * lax.rem(lax.div(index, bit), 2)
    return index


def split_dot(a, b):
    high = a.astype(jnp.bfloat16)
    low = (a - high.astype(jnp.float32)).astype(jnp.bfloat16)
    return jnp.dot(high, b, preferred_element_type=jnp.float32) + jnp.dot(
        low, b, preferred_element_type=jnp.float32
    )


def exact_dot(a, b):
    return jnp.dot(a, b, precision=lax.Precision.HIGHEST, preferred_element_type=jnp.float32)


def fused_kernel(
    tokens_in, gain_in, count_in, owners_in, targets_in, kept_in, w_query, w_keyvalue, cache,
    attended, compacted,
    tokens, gain, count, owners, targets, kept_rows, weight, pages, rows, leaving, projected, local, planes, fresh, sums, peaks,
    load_sem, keep_sem, row_send, row_recv, page_send, page_recv, proj_send, proj_recv,
    query_send, query_recv, fresh_send, fresh_recv, sum_send, sum_recv, peak_send, peak_recv,
):
    p = lax.axis_index("page")
    t = lax.axis_index("tensor")
    part = rows.shape[2]
    requests = part * HOLDERS
    slots = leaving.shape[0]
    keep = leaving.shape[1]
    cap = slots // HOLDERS
    page_rows = cache.shape[0] // slots

    loads = [
        pltpu.make_async_copy(tokens_in.at[p], tokens, load_sem.at[3]),
        pltpu.make_async_copy(gain_in, gain, load_sem.at[4]),
        pltpu.make_async_copy(count_in, count, load_sem.at[5]),
        pltpu.make_async_copy(owners_in, owners, load_sem.at[6]),
        pltpu.make_async_copy(targets_in, targets, load_sem.at[7]),
        pltpu.make_async_copy(kept_in, kept_rows, load_sem.at[8]),
        pltpu.make_async_copy(cache, pages, load_sem.at[0]),
        pltpu.make_async_copy(w_query, weight.at[pl.ds(0, 320)], load_sem.at[1]),
        pltpu.make_async_copy(w_keyvalue, weight.at[pl.ds(320, 160)], load_sem.at[2]),
    ]
    for load in loads:
        load.start()

    barrier = pltpu.get_barrier_semaphore()
    for f in range(1, GROUPS):
        pl.semaphore_signal(barrier, inc=1, device_id=(p, partner(t, f)), device_id_type=MESH)
    for f in range(1, HOLDERS):
        pl.semaphore_signal(barrier, inc=1, device_id=(partner(p, f), t), device_id_type=MESH)

    weight[480:512] = jnp.zeros((32, weight.shape[1]), weight.dtype)
    loads[0].wait()
    loads[1].wait()
    gains = gain[...]
    gains = jnp.concatenate([gains[i : i + 1] for i in range(gains.shape[0])], axis=1)
    mine = tokens[...].astype(jnp.float32)
    square = jnp.mean(mine * mine, axis=-1, keepdims=True)
    normed = (mine * lax.rsqrt(square + EPSILON) * gains).astype(jnp.bfloat16)
    half = normed.shape[1] // 2
    rows[0, 0] = normed[:, :half]
    rows[1, 0] = normed[:, half:]
    pl.semaphore_wait(barrier, GROUPS + HOLDERS - 2)

    def pass_row(h, e, f):
        copy = pltpu.make_async_remote_copy(
            src_ref=rows.at[h, e],
            dst_ref=rows.at[h, e ^ f],
            send_sem=row_send.at[h, e ^ f],
            recv_sem=row_recv.at[h, e ^ f],
            device_id=(p, partner(t, f)),
            device_id_type=MESH,
        )
        copy.start()
        return copy

    moved = {}
    for h in range(2):
        for f in (4, 2, 1):
            moved[h, f] = pass_row(h, 0, f)

    def forward(h, e):
        moved[h, e].wait_recv()
        if e == 4:
            moved[h, 6] = pass_row(h, 4, 2)
        if (h, e) == (1, 5):
            moved[h, 7] = pass_row(h, 5, 2)
        elif (h, e) != (1, 6):
            moved[h, e + 1] = pass_row(h, e, 1)

    for load in loads[2:6]:
        load.wait()
    live = lax.broadcasted_iota(jnp.int32, (1, slots), 1) < count[...]
    target = jnp.where(live, targets[...], -1)
    owner_plus = owners[...].astype(jnp.float32) + 1.0

    def tags_of(shape, shift):
        at = lax.broadcasted_iota(jnp.int32, shape, 0) >> shift
        return jnp.sum(jnp.where(target == at, owner_plus, 0.0), axis=1, keepdims=True) - 1.0

    pairs = slots * KV_HEADS
    tags = tags_of((slots, slots), 0)
    tag_rows = tags_of((pairs, slots), 3)
    picks = jnp.concatenate([kept_rows[s] for s in range(slots)], axis=0).astype(jnp.float32)
    placed = (slots * keep, keep)
    repeat_rows = jnp.where(
        (lax.broadcasted_iota(jnp.int32, placed, 0) & (keep - 1))
        == lax.broadcasted_iota(jnp.int32, placed, 1),
        1.0,
        0.0,
    )
    code = lax.dot_general(
        repeat_rows.astype(jnp.bfloat16),
        picks.astype(jnp.bfloat16),
        (((1,), (1,)), ((), ())),
        preferred_element_type=jnp.float32,
    )
    at = lax.broadcasted_iota(jnp.int32, (slots * keep, slots), 0) >> 5
    code = jnp.where(target == at, code, -1.0)
    lane = lax.broadcasted_iota(jnp.int32, (slots * keep, page_rows), 1).astype(jnp.float32)
    choice = jnp.concatenate(
        [jnp.where(code[:, s : s + 1] == lane, 1.0, 0.0).astype(jnp.bfloat16) for s in range(slots)],
        axis=1,
    )
    loads[6].wait()
    forward(0, 4)
    forward(0, 2)
    left = jnp.dot(choice, pages[:, :PLANE], preferred_element_type=jnp.float32)
    forward(1, 4)
    forward(1, 2)
    right = jnp.dot(choice, pages[:, PLANE:], preferred_element_type=jnp.float32)
    out = jnp.concatenate([left, right], axis=1).astype(jnp.bfloat16)
    leaving[...] = out.reshape(leaving.shape)
    page_copies = []
    for f in range(1, HOLDERS):
        copy = pltpu.make_async_remote_copy(
            src_ref=leaving.at[pl.ds(partner(p, f) * cap, cap)],
            dst_ref=compacted.at[pl.ds(p * cap, cap)],
            send_sem=page_send.at[f],
            recv_sem=page_recv.at[f],
            device_id=(partner(p, f), t),
            device_id_type=MESH,
        )
        copy.start()
        page_copies.append(copy)
    kept = pltpu.make_async_copy(
        leaving.at[pl.ds(p * cap, cap)], compacted.at[pl.ds(p * cap, cap)], keep_sem
    )
    kept.start()

    loads[7].wait()
    loads[8].wait()
    forward(0, 6)
    forward(1, 5)
    forward(1, 6)

    def project(first):
        both = 0.0
        for h in range(2):
            if first == 1:
                for e in (1, 3, 5, 7):
                    if (h, e) != (1, 5):
                        moved[h, e].wait_recv()
            both += lax.dot_general(
                jnp.concatenate([rows[h, e] for e in range(first, GROUPS, 2)], axis=0),
                weight[:, h * half : (h + 1) * half],
                (((1,), (1,)), ((), ())),
                preferred_element_type=jnp.float32,
            )
        both = both.astype(jnp.bfloat16)
        copies = []
        for n, e in enumerate(range(first, GROUPS, 2)):
            block = both[n * part : (n + 1) * part]
            if e == 0:
                local[t] = block
                continue
            projected[e] = block
            copy = pltpu.make_async_remote_copy(
                src_ref=projected.at[e],
                dst_ref=local.at[t],
                send_sem=proj_send.at[e],
                recv_sem=proj_recv.at[e],
                device_id=(p, partner(t, e)),
                device_id_type=MESH,
            )
            copy.start()
            copies.append(copy)
        return copies

    proj_copies = project(0)
    proj_copies += project(1)
    for copy in proj_copies:
        copy.wait_recv()

    blocks = [local[g].astype(jnp.float32) for g in range(GROUPS)]
    for k in range(REPEAT):
        planes[p, k] = jnp.concatenate(
            [b[:, k * HEAD_DIM : (k + 1) * HEAD_DIM] for b in blocks], axis=1
        ).astype(jnp.bfloat16)
    for n in range(2):
        fresh[p, n] = jnp.concatenate(
            [b[:, 320:480] for b in blocks[4 * n : 4 * n + 4]], axis=1
        ).astype(jnp.bfloat16)

    def to_holders(ref_of, send, recv):
        copies = []
        for f in range(1, HOLDERS):
            copy = pltpu.make_async_remote_copy(
                src_ref=ref_of(),
                dst_ref=ref_of(),
                send_sem=send.at[f],
                recv_sem=recv.at[f],
                device_id=(partner(p, f), t),
                device_id_type=MESH,
            )
            copy.start()
            copies.append(copy)
        return copies

    query_copies = to_holders(lambda: planes.at[p], query_send, query_recv)
    fresh_copies = to_holders(lambda: fresh.at[p], fresh_send, fresh_recv)

    def plane(ref, k):
        return jnp.concatenate([ref[h, k] for h in range(HOLDERS)], axis=0)

    member_row = jnp.where(
        tag_rows == lax.broadcasted_iota(jnp.int32, (pairs, requests), 1).astype(jnp.float32),
        1.0,
        0.0,
    ).astype(jnp.bfloat16)
    own_head = head_of((pairs, PLANE), 1) == (
        lax.broadcasted_iota(jnp.int32, (pairs, PLANE), 0) & (KV_HEADS - 1)
    )
    slot_rows = leaving[...].reshape(slots * keep, 2 * PLANE)
    for copy in query_copies:
        copy.wait_recv()

    spread = []
    for k in range(REPEAT):
        q = plane(planes, k)
        found = jnp.dot(member_row, q, preferred_element_type=jnp.float32)
        spread.append(jnp.where(own_head, found, 0.0).astype(jnp.bfloat16))
    scores = SCALE * lax.dot_general(
        jnp.concatenate(spread, axis=0),
        slot_rows[:, :PLANE],
        (((1,), (1,)), ((), ())),
        preferred_element_type=jnp.float32,
    )
    full = (REPEAT * pairs, slots * keep)
    same = ((lax.broadcasted_iota(jnp.int32, full, 0) >> 3) & (slots - 1)) == (
        lax.broadcasted_iota(jnp.int32, full, 1) >> 5
    )
    scores = jnp.where(same, scores, NEGATIVE)
    peak = jnp.max(scores, axis=1, keepdims=True)
    weights = jnp.where(same, jnp.exp(scores - peak), 0.0)
    total = jnp.sum(weights, axis=1, keepdims=True)
    mixed = jnp.dot(
        weights.astype(jnp.bfloat16), slot_rows[:, PLANE:], preferred_element_type=jnp.float32
    ) * (1.0 / total)
    mixed = mixed.reshape(REPEAT, pairs, PLANE)
    mixed = jnp.where(own_head[None], mixed, 0.0).astype(jnp.bfloat16)
    gather = (REPEAT * slots, REPEAT * pairs)
    of_slot = lax.broadcasted_iota(jnp.int32, gather, 0) == (
        lax.broadcasted_iota(jnp.int32, gather, 1) >> 3
    )
    sums[p] = jnp.dot(
        jnp.where(of_slot, 1.0, 0.0).astype(jnp.bfloat16),
        mixed.reshape(REPEAT * pairs, PLANE),
        preferred_element_type=jnp.float32,
    ).astype(jnp.bfloat16)
    lse = peak + jnp.log(total)
    wide = (REPEAT * pairs, 128)
    row_id = lax.broadcasted_iota(jnp.int32, wide, 0)
    at = (row_id >> 6) * KV_HEADS + (row_id & (KV_HEADS - 1))
    lse = jnp.where(lax.broadcasted_iota(jnp.int32, wide, 1) == at, lse, 0.0)
    lse = jnp.sum(lse.reshape(REPEAT, slots, KV_HEADS, 128), axis=2)
    lse = lse[0] + lse[1] + lse[2] + lse[3]
    peaks[p] = jnp.where(
        lax.broadcasted_iota(jnp.int32, (slots, 128), 1) == 127, tags, lse
    )
    peak_copies = to_holders(lambda: peaks.at[p], peak_send, peak_recv)
    sum_copies = to_holders(lambda: sums.at[p], sum_send, sum_recv)

    for copy in fresh_copies:
        copy.wait_recv()
    new_keys = plane(fresh, 0).astype(jnp.float32)
    new_values = plane(fresh, 1).astype(jnp.float32)
    own = jnp.zeros((requests, 128), jnp.float32)
    segment_head = head_of((PLANE, 128), 0)
    segment_lane = lax.broadcasted_iota(jnp.int32, (PLANE, 128), 1)
    for k in range(REPEAT):
        q = plane(planes, k).astype(jnp.float32)
        segment = jnp.where(segment_lane == segment_head + k * KV_HEADS, 1.0, 0.0)
        own += split_dot(q * new_keys, segment.astype(jnp.bfloat16))
    own = own * SCALE

    for copy in peak_copies:
        copy.wait_recv()
    every = HOLDERS * slots
    lse = peaks[...].reshape(every, 128)
    owner = lse[:, 127:128]
    where_slot = lax.broadcasted_iota(jnp.int32, (every, every), 0)
    where_lane = lax.broadcasted_iota(jnp.int32, (every, every), 1)
    owner_row = jnp.sum(jnp.where(where_slot == where_lane, owner, 0.0), axis=0, keepdims=True)
    request = lax.broadcasted_iota(jnp.int32, (requests, every), 0).astype(jnp.float32)
    member = jnp.where(request == owner_row, 1.0, 0.0)
    request = lax.broadcasted_iota(jnp.int32, (every, requests), 1).astype(jnp.float32)
    slot_member = jnp.where(request == owner, 1.0, 0.0)
    top = own
    for s in range(every):
        top = jnp.maximum(top, jnp.where(member[:, s : s + 1] > 0.0, lse[s : s + 1], NEGATIVE))
    factor = jnp.exp(lse - exact_dot(slot_member, top))
    factor = jnp.where(owner >= 0.0, factor, 0.0)
    own_weight = jnp.exp(own - top)
    whole = exact_dot(member, factor) + own_weight
    slot_whole = exact_dot(slot_member, whole)
    slot_part = factor / jnp.where(owner >= 0.0, slot_whole, 1.0)
    own_part = own_weight / whole
    parts = jnp.concatenate([slot_part, own_part], axis=0)

    for copy in sum_copies:
        copy.wait_recv()
    slot_sums = sums[...].astype(jnp.float32).reshape(HOLDERS, REPEAT, slots, PLANE)
    member = member.astype(jnp.bfloat16)
    spread_head = head_of((128, PLANE), 1)
    spread_row = lax.broadcasted_iota(jnp.int32, (128, PLANE), 0)
    results = []
    for k in range(REPEAT):
        expand = jnp.where(spread_row == spread_head + k * KV_HEADS, 1.0, 0.0)
        shares = split_dot(parts, expand.astype(jnp.bfloat16))
        weighted = (shares[:every] * slot_sums[:, k].reshape(every, PLANE)).astype(jnp.bfloat16)
        results.append(
            jnp.dot(member, weighted, preferred_element_type=jnp.float32)
            + shares[every:] * new_values
        )
    attended[...] = jnp.concatenate(
        [
            results[k][:, g * HEAD_DIM : (g + 1) * HEAD_DIM]
            for g in range(KV_HEADS)
            for k in range(REPEAT)
        ],
        axis=1,
    ).astype(jnp.bfloat16)

    for copy in page_copies:
        copy.wait_recv()
    kept.wait()
    for copy in (
        list(moved.values()) + page_copies + proj_copies + query_copies + fresh_copies
        + peak_copies + sum_copies
    ):
        copy.wait_send()


def fused_device(
    tokens, norm_gain, w_query, w_keyvalue, cache, page_count, page_owner, keep_rows, dest_slot
):
    slots, _, page_rows, width = cache.shape
    keep = keep_rows.shape[2]
    requests, model = tokens.shape
    part = requests // HOLDERS
    vmem = pl.BlockSpec(memory_space=pltpu.VMEM)
    pinned = pl.BlockSpec(memory_space=pltpu.HBM)
    bf16, f32 = jnp.bfloat16, jnp.float32
    dma = pltpu.SemaphoreType.DMA
    attended, compacted = pl.pallas_call(
        fused_kernel,
        out_shape=(
            jax.ShapeDtypeStruct((requests, HEADS * HEAD_DIM), bf16),
            jax.ShapeDtypeStruct((slots, keep, width), bf16),
        ),
        in_specs=[pinned] * 9,
        out_specs=(vmem, vmem),
        scratch_shapes=[
            pltpu.VMEM((part, model), bf16),
            pltpu.VMEM((model // 128, 128), f32),
            pltpu.VMEM((1, 1), jnp.int32),
            pltpu.VMEM((1, slots), jnp.int32),
            pltpu.VMEM((1, slots), jnp.int32),
            pltpu.VMEM(keep_rows.shape, jnp.int32),
            pltpu.VMEM((512, model), bf16),
            pltpu.VMEM((slots * page_rows, width), bf16),
            pltpu.VMEM((2, GROUPS, part, model // 2), bf16),
            pltpu.VMEM((slots, keep, width), bf16),
            pltpu.VMEM((GROUPS, part, 512), bf16),
            pltpu.VMEM((GROUPS, part, 512), bf16),
            pltpu.VMEM((HOLDERS, REPEAT, part, PLANE), bf16),
            pltpu.VMEM((HOLDERS, 2, part, PLANE), bf16),
            pltpu.VMEM((HOLDERS, REPEAT * slots, PLANE), bf16),
            pltpu.VMEM((HOLDERS, slots, 128), f32),
            dma((9,)),
            dma,
            dma((2, GROUPS)),
            dma((2, GROUPS)),
            dma((HOLDERS,)),
            dma((HOLDERS,)),
            dma((GROUPS,)),
            dma((GROUPS,)),
        ]
        + [dma((HOLDERS,))] * 8,
        compiler_params=pltpu.CompilerParams(
            collective_id=0, has_side_effects=True, vmem_limit_bytes=48 * 1024 * 1024
        ),
        cost_estimate=pl.CostEstimate(
            flops=1_500_000_000, bytes_accessed=7_000_000, transcendentals=70_000
        ),
    )(
        tokens.reshape(HOLDERS, part, model),
        norm_gain.reshape(model // 128, 128),
        page_count,
        page_owner.reshape(1, slots),
        dest_slot.reshape(1, slots),
        keep_rows,
        w_query.T,
        w_keyvalue.T,
        cache.reshape(slots * page_rows, width),
    )
    return attended, compacted[:, None]


def local_step(sizes, tokens, norm_gain, w_query, w_keyvalue, cache, *rest):
    fits = (
        sizes == {"page": HOLDERS, "tensor": GROUPS}
        and tokens.shape[0] == 64
        and cache.shape[0] == 8
        and rest[2].shape[2] == 32
    )
    step = fused_device if fits else per_device
    return step(tokens, norm_gain, w_query, w_keyvalue, cache, *rest)


def solution(mesh):
    return jax.shard_map(
        functools.partial(local_step, dict(mesh.shape)),
        mesh=mesh,
        in_specs=(
            P("tensor", None),
            P(),
            P(None, "tensor"),
            P(None, "tensor"),
            P("page", "tensor", None, None),
            P("page", "tensor"),
            P("page", "tensor"),
            P("page", "tensor", None),
            P("page", "tensor"),
        ),
        out_specs=(P("tensor", None), P("page", "tensor", None, None)),
        check_vma=False,
    )
```

```python
import functools

import jax
import jax.numpy as jnp
from jax import lax
from jax.experimental import pallas as pl
from jax.experimental.pallas import tpu as pltpu
from jax.sharding import PartitionSpec as P

HEADS = 32
KV_HEADS = 8
HEAD_DIM = 80


EPSILON = 1e-05
NEGATIVE = -1e30


def per_device(
    tokens, norm_gain, w_query, w_keyvalue, cache, page_count, page_owner, keep_rows, dest_slot
):
    holders = lax.axis_size("page")
    groups = lax.axis_size("tensor")
    rows_here = tokens.shape[0]
    sources = cache.shape[0]
    keep_count = keep_rows.shape[2]
    row_width = cache.shape[3]
    capacity = (sources + holders - 1) // holders
    targets = capacity * holders
    repeat_count = HEADS // KV_HEADS
    score_scale = HEAD_DIM ** (-0.5)
    widened = tokens.astype(jnp.float32)
    normed = (
        widened
        * lax.rsqrt(jnp.mean(widened * widened, axis=-1, keepdims=True) + EPSILON)
        * norm_gain
    ).astype(jnp.bfloat16)
    portion = lax.all_gather(normed, "tensor", axis=0, tiled=True)
    query_part = jnp.dot(portion, w_query, preferred_element_type=jnp.float32)
    pair_part = jnp.dot(portion, w_keyvalue, preferred_element_type=jnp.float32)
    projected = jnp.concatenate([query_part, pair_part], axis=1).astype(jnp.bfloat16)
    local_heads = lax.all_to_all(
        projected, "tensor", split_axis=0, concat_axis=1, tiled=True
    ).reshape(rows_here, groups, -1)
    query_cols = w_query.shape[1]
    queries = local_heads[:, :, :query_cols].reshape(rows_here, KV_HEADS, repeat_count, HEAD_DIM)
    fresh_kv = local_heads[:, :, query_cols:].reshape(rows_here, 2, KV_HEADS, HEAD_DIM)
    new_keys = fresh_kv[:, 0]
    new_values = fresh_kv[:, 1]
    retained = jax.vmap(lambda one_page, row_picks: one_page[row_picks])(
        cache[:, 0], keep_rows[:, 0]
    )
    is_live = jnp.arange(sources) < page_count[0, 0]
    owners = page_owner[:, 0]
    chosen = (dest_slot[:, 0][None, :] == jnp.arange(targets)[:, None]) & is_live[None, :]
    outgoing = jnp.einsum(
        "ts,sjc->tjc", chosen.astype(jnp.bfloat16), retained, preferred_element_type=jnp.float32
    ).astype(jnp.bfloat16)
    out_tags = jnp.sum(jnp.where(chosen, owners[None, :] + 1, 0), axis=1) - 1
    arrived, arrived_tags = (
        lax.all_to_all(
            outgoing.reshape(holders, capacity, keep_count, row_width),
            "page",
            split_axis=0,
            concat_axis=0,
            tiled=True,
        ),
        lax.all_to_all(
            out_tags.reshape(holders, capacity), "page", split_axis=0, concat_axis=0, tiled=True
        ),
    )
    arrived = arrived.reshape(targets, keep_count, row_width)
    arrived_tags = arrived_tags.reshape(targets)
    slot_count = arrived.shape[0]
    active = arrived_tags >= 0
    owner_idx = jnp.maximum(arrived_tags, 0)
    picked = jnp.take(queries, owner_idx, axis=0)
    slot_keys = arrived[:, :, : KV_HEADS * HEAD_DIM].reshape(
        slot_count, keep_count, KV_HEADS, HEAD_DIM
    )
    slot_values = arrived[:, :, KV_HEADS * HEAD_DIM :].reshape(
        slot_count, keep_count, KV_HEADS, HEAD_DIM
    )
    scores = (
        jnp.einsum("sgkd,sjgd->sgkj", picked, slot_keys, preferred_element_type=jnp.float32)
        * score_scale
    )
    member = (owner_idx[None, :] == jnp.arange(rows_here)[:, None]) & active[None, :]
    slot_peak = jnp.max(scores, axis=3)
    local_peak = jnp.max(jnp.where(member[:, :, None, None], slot_peak[None], NEGATIVE), axis=1)
    own_score = (
        jnp.einsum("rgkd,rgd->rgk", queries, new_keys, preferred_element_type=jnp.float32)
        * score_scale
    )
    row_peak = jnp.maximum(lax.pmax(local_peak, "page"), own_score)
    shifted = scores - jnp.take(row_peak, owner_idx, axis=0)[..., None]
    weights = jnp.where(active[:, None, None, None], jnp.exp(shifted), 0.0)
    slot_total = jnp.sum(weights, axis=3)
    slot_out = jnp.einsum(
        "sgkj,sjgd->sgkd",
        weights.astype(jnp.bfloat16),
        slot_values,
        preferred_element_type=jnp.float32,
    )
    member_weight = member.astype(jnp.float32)
    part_total = jnp.einsum(
        "rs,sgk->rgk", member_weight, slot_total, precision=lax.Precision.HIGHEST
    )
    part_out = jnp.einsum("rs,sgkd->rgkd", member_weight, slot_out, precision=lax.Precision.HIGHEST)
    sum_out, sum_total = lax.psum((part_out, part_total), "page")
    own_weight = jnp.exp(own_score - row_peak)
    mixed = sum_out + own_weight[..., None] * new_values[:, :, None, :].astype(jnp.float32)
    result = mixed / (sum_total + own_weight)[..., None]
    return (result.reshape(rows_here, HEADS * HEAD_DIM).astype(jnp.bfloat16), arrived[:, None])


MESH = pl.DeviceIdType.MESH
SCALE = HEAD_DIM ** (-0.5)
REPEAT = HEADS // KV_HEADS
PLANE = KV_HEADS * HEAD_DIM
HOLDERS, GROUPS = 4, 8


def head_of(shape, axis):
    return (lax.broadcasted_iota(jnp.int32, shape, axis) * 3277) >> 18


def partner(index, flip):
    for bit in (1, 2, 4):
        if flip & bit:
            index = index + bit - 2 * bit * lax.rem(lax.div(index, bit), 2)
    return index


def split_dot(a, b):
    high = a.astype(jnp.bfloat16)
    low = (a - high.astype(jnp.float32)).astype(jnp.bfloat16)
    return jnp.dot(high, b, preferred_element_type=jnp.float32) + jnp.dot(
        low, b, preferred_element_type=jnp.float32
    )


def exact_dot(a, b):
    return jnp.dot(a, b, precision=lax.Precision.HIGHEST, preferred_element_type=jnp.float32)


def fused_kernel(
    tokens_in, gain_in, count_in, owners_in, targets_in, kept_in, w_query, w_keyvalue, cache,
    attended, compacted,
    tokens, gain, count, owners, targets, kept_rows, weight, pages, rows, leaving, projected, local, planes, fresh, sums, peaks,
    load_sem, keep_sem, row_send, row_recv, page_send, page_recv, proj_send, proj_recv,
    query_send, query_recv, fresh_send, fresh_recv, sum_send, sum_recv, peak_send, peak_recv,
):
    p = lax.axis_index("page")
    t = lax.axis_index("tensor")
    part = rows.shape[2]
    requests = part * HOLDERS
    slots = leaving.shape[0]
    keep = leaving.shape[1]
    cap = slots // HOLDERS
    page_rows = cache.shape[0] // slots

    loads = [
        pltpu.make_async_copy(tokens_in.at[p], tokens, load_sem.at[3]),
        pltpu.make_async_copy(gain_in, gain, load_sem.at[4]),
        pltpu.make_async_copy(count_in, count, load_sem.at[5]),
        pltpu.make_async_copy(owners_in, owners, load_sem.at[6]),
        pltpu.make_async_copy(targets_in, targets, load_sem.at[7]),
        pltpu.make_async_copy(kept_in, kept_rows, load_sem.at[8]),
        pltpu.make_async_copy(cache, pages, load_sem.at[0]),
        pltpu.make_async_copy(w_query, weight.at[pl.ds(0, 320)], load_sem.at[1]),
        pltpu.make_async_copy(w_keyvalue, weight.at[pl.ds(320, 160)], load_sem.at[2]),
    ]
    for load in loads:
        load.start()

    barrier = pltpu.get_barrier_semaphore()
    for f in range(1, GROUPS):
        pl.semaphore_signal(barrier, inc=1, device_id=(p, partner(t, f)), device_id_type=MESH)
    for f in range(1, HOLDERS):
        pl.semaphore_signal(barrier, inc=1, device_id=(partner(p, f), t), device_id_type=MESH)

    weight[480:512] = jnp.zeros((32, weight.shape[1]), weight.dtype)
    loads[0].wait()
    loads[1].wait()
    gains = gain[...]
    gains = jnp.concatenate([gains[i : i + 1] for i in range(gains.shape[0])], axis=1)
    mine = tokens[...].astype(jnp.float32)
    square = jnp.mean(mine * mine, axis=-1, keepdims=True)
    normed = (mine * lax.rsqrt(square + EPSILON) * gains).astype(jnp.bfloat16)
    half = normed.shape[1] // 2
    rows[0, 0] = normed[:, :half]
    rows[1, 0] = normed[:, half:]
    pl.semaphore_wait(barrier, GROUPS + HOLDERS - 2)

    def pass_row(h, e, f):
        copy = pltpu.make_async_remote_copy(
            src_ref=rows.at[h, e],
            dst_ref=rows.at[h, e ^ f],
            send_sem=row_send.at[h, e ^ f],
            recv_sem=row_recv.at[h, e ^ f],
            device_id=(p, partner(t, f)),
            device_id_type=MESH,
        )
        copy.start()
        return copy

    moved = {}
    for h in range(2):
        for f in (4, 2, 1):
            moved[h, f] = pass_row(h, 0, f)

    def forward(h, e):
        moved[h, e].wait_recv()
        if e == 4:
            moved[h, 6] = pass_row(h, 4, 2)
        if (h, e) == (1, 5):
            moved[h, 7] = pass_row(h, 5, 2)
        elif (h, e) != (1, 6):
            moved[h, e + 1] = pass_row(h, e, 1)

    for load in loads[2:6]:
        load.wait()
    live = lax.broadcasted_iota(jnp.int32, (1, slots), 1) < count[...]
    target = jnp.where(live, targets[...], -1)
    owner_plus = owners[...].astype(jnp.float32) + 1.0

    def tags_of(shape, shift):
        at = lax.broadcasted_iota(jnp.int32, shape, 0) >> shift
        return jnp.sum(jnp.where(target == at, owner_plus, 0.0), axis=1, keepdims=True) - 1.0

    pairs = slots * KV_HEADS
    tags = tags_of((slots, slots), 0)
    tag_rows = tags_of((pairs, slots), 3)
    picks = jnp.concatenate([kept_rows[s] for s in range(slots)], axis=0).astype(jnp.float32)
    placed = (slots * keep, keep)
    repeat_rows = jnp.where(
        (lax.broadcasted_iota(jnp.int32, placed, 0) & (keep - 1))
        == lax.broadcasted_iota(jnp.int32, placed, 1),
        1.0,
        0.0,
    )
    code = lax.dot_general(
        repeat_rows.astype(jnp.bfloat16),
        picks.astype(jnp.bfloat16),
        (((1,), (1,)), ((), ())),
        preferred_element_type=jnp.float32,
    )
    at = lax.broadcasted_iota(jnp.int32, (slots * keep, slots), 0) >> 5
    code = jnp.where(target == at, code, -1.0)
    lane = lax.broadcasted_iota(jnp.int32, (slots * keep, page_rows), 1).astype(jnp.float32)
    choice = jnp.concatenate(
        [jnp.where(code[:, s : s + 1] == lane, 1.0, 0.0).astype(jnp.bfloat16) for s in range(slots)],
        axis=1,
    )
    loads[6].wait()
    forward(0, 4)
    forward(0, 2)
    left = jnp.dot(choice, pages[:, :PLANE], preferred_element_type=jnp.float32)
    forward(1, 4)
    forward(1, 2)
    right = jnp.dot(choice, pages[:, PLANE:], preferred_element_type=jnp.float32)
    out = jnp.concatenate([left, right], axis=1).astype(jnp.bfloat16)
    leaving[...] = out.reshape(leaving.shape)
    page_copies = []
    for f in range(1, HOLDERS):
        copy = pltpu.make_async_remote_copy(
            src_ref=leaving.at[pl.ds(partner(p, f) * cap, cap)],
            dst_ref=compacted.at[pl.ds(p * cap, cap)],
            send_sem=page_send.at[f],
            recv_sem=page_recv.at[f],
            device_id=(partner(p, f), t),
            device_id_type=MESH,
        )
        copy.start()
        page_copies.append(copy)
    kept = pltpu.make_async_copy(
        leaving.at[pl.ds(p * cap, cap)], compacted.at[pl.ds(p * cap, cap)], keep_sem
    )
    kept.start()

    loads[7].wait()
    loads[8].wait()
    forward(0, 6)
    forward(1, 5)
    forward(1, 6)

    def project(first):
        both = 0.0
        for h in range(2):
            if first == 1:
                for e in (1, 3, 5, 7):
                    if (h, e) != (1, 5):
                        moved[h, e].wait_recv()
            both += lax.dot_general(
                jnp.concatenate([rows[h, e] for e in range(first, GROUPS, 2)], axis=0),
                weight[:, h * half : (h + 1) * half],
                (((1,), (1,)), ((), ())),
                preferred_element_type=jnp.float32,
            )
        both = both.astype(jnp.bfloat16)
        copies = []
        for n, e in enumerate(range(first, GROUPS, 2)):
            block = both[n * part : (n + 1) * part]
            if e == 0:
                local[t] = block
                continue
            projected[e] = block
            copy = pltpu.make_async_remote_copy(
                src_ref=projected.at[e],
                dst_ref=local.at[t],
                send_sem=proj_send.at[e],
                recv_sem=proj_recv.at[e],
                device_id=(p, partner(t, e)),
                device_id_type=MESH,
            )
            copy.start()
            copies.append(copy)
        return copies

    proj_copies = project(0)
    proj_copies += project(1)
    for copy in proj_copies:
        copy.wait_recv()

    blocks = [local[g].astype(jnp.float32) for g in range(GROUPS)]
    for k in range(REPEAT):
        planes[p, k] = jnp.concatenate(
            [b[:, k * HEAD_DIM : (k + 1) * HEAD_DIM] for b in blocks], axis=1
        ).astype(jnp.bfloat16)
    for n in range(2):
        fresh[p, n] = jnp.concatenate(
            [b[:, 320:480] for b in blocks[4 * n : 4 * n + 4]], axis=1
        ).astype(jnp.bfloat16)

    def to_holders(ref_of, send, recv):
        copies = []
        for f in range(1, HOLDERS):
            copy = pltpu.make_async_remote_copy(
                src_ref=ref_of(),
                dst_ref=ref_of(),
                send_sem=send.at[f],
                recv_sem=recv.at[f],
                device_id=(partner(p, f), t),
                device_id_type=MESH,
            )
            copy.start()
            copies.append(copy)
        return copies

    query_copies = to_holders(lambda: planes.at[p], query_send, query_recv)
    fresh_copies = to_holders(lambda: fresh.at[p], fresh_send, fresh_recv)

    def plane(ref, k):
        return jnp.concatenate([ref[h, k] for h in range(HOLDERS)], axis=0)

    member_row = jnp.where(
        tag_rows == lax.broadcasted_iota(jnp.int32, (pairs, requests), 1).astype(jnp.float32),
        1.0,
        0.0,
    ).astype(jnp.bfloat16)
    own_head = head_of((pairs, PLANE), 1) == (
        lax.broadcasted_iota(jnp.int32, (pairs, PLANE), 0) & (KV_HEADS - 1)
    )
    slot_rows = leaving[...].reshape(slots * keep, 2 * PLANE)
    for copy in query_copies:
        copy.wait_recv()

    spread = []
    for k in range(REPEAT):
        q = plane(planes, k)
        found = jnp.dot(member_row, q, preferred_element_type=jnp.float32)
        spread.append(jnp.where(own_head, found, 0.0).astype(jnp.bfloat16))
    scores = SCALE * lax.dot_general(
        jnp.concatenate(spread, axis=0),
        slot_rows[:, :PLANE],
        (((1,), (1,)), ((), ())),
        preferred_element_type=jnp.float32,
    )
    full = (REPEAT * pairs, slots * keep)
    same = ((lax.broadcasted_iota(jnp.int32, full, 0) >> 3) & (slots - 1)) == (
        lax.broadcasted_iota(jnp.int32, full, 1) >> 5
    )
    scores = jnp.where(same, scores, NEGATIVE)
    peak = jnp.max(scores, axis=1, keepdims=True)
    weights = jnp.where(same, jnp.exp(scores - peak), 0.0)
    total = jnp.sum(weights, axis=1, keepdims=True)
    mixed = jnp.dot(
        weights.astype(jnp.bfloat16), slot_rows[:, PLANE:], preferred_element_type=jnp.float32
    ) * (1.0 / total)
    mixed = mixed.reshape(REPEAT, pairs, PLANE)
    mixed = jnp.where(own_head[None], mixed, 0.0).astype(jnp.bfloat16)
    gather = (REPEAT * slots, REPEAT * pairs)
    of_slot = lax.broadcasted_iota(jnp.int32, gather, 0) == (
        lax.broadcasted_iota(jnp.int32, gather, 1) >> 3
    )
    sums[p] = jnp.dot(
        jnp.where(of_slot, 1.0, 0.0).astype(jnp.bfloat16),
        mixed.reshape(REPEAT * pairs, PLANE),
        preferred_element_type=jnp.float32,
    ).astype(jnp.bfloat16)
    lse = peak + jnp.log(total)
    wide = (REPEAT * pairs, 128)
    row_id = lax.broadcasted_iota(jnp.int32, wide, 0)
    at = (row_id >> 6) * KV_HEADS + (row_id & (KV_HEADS - 1))
    lse = jnp.where(lax.broadcasted_iota(jnp.int32, wide, 1) == at, lse, 0.0)
    lse = jnp.sum(lse.reshape(REPEAT, slots, KV_HEADS, 128), axis=2)
    lse = lse[0] + lse[1] + lse[2] + lse[3]
    peaks[p] = jnp.where(
        lax.broadcasted_iota(jnp.int32, (slots, 128), 1) == 127, tags, lse
    )
    peak_copies = to_holders(lambda: peaks.at[p], peak_send, peak_recv)
    sum_copies = to_holders(lambda: sums.at[p], sum_send, sum_recv)

    for copy in fresh_copies:
        copy.wait_recv()
    new_keys = plane(fresh, 0).astype(jnp.float32)
    new_values = plane(fresh, 1).astype(jnp.float32)
    own = jnp.zeros((requests, 128), jnp.float32)
    segment_head = head_of((PLANE, 128), 0)
    segment_lane = lax.broadcasted_iota(jnp.int32, (PLANE, 128), 1)
    for k in range(REPEAT):
        q = plane(planes, k).astype(jnp.float32)
        segment = jnp.where(segment_lane == segment_head + k * KV_HEADS, 1.0, 0.0)
        own += split_dot(q * new_keys, segment.astype(jnp.bfloat16))
    own = own * SCALE

    for copy in peak_copies:
        copy.wait_recv()
    every = HOLDERS * slots
    lse = peaks[...].reshape(every, 128)
    owner = lse[:, 127:128]
    where_slot = lax.broadcasted_iota(jnp.int32, (every, every), 0)
    where_lane = lax.broadcasted_iota(jnp.int32, (every, every), 1)
    owner_row = jnp.sum(jnp.where(where_slot == where_lane, owner, 0.0), axis=0, keepdims=True)
    request = lax.broadcasted_iota(jnp.int32, (requests, every), 0).astype(jnp.float32)
    member = jnp.where(request == owner_row, 1.0, 0.0)
    request = lax.broadcasted_iota(jnp.int32, (every, requests), 1).astype(jnp.float32)
    slot_member = jnp.where(request == owner, 1.0, 0.0)
    top = own
    for s in range(every):
        top = jnp.maximum(top, jnp.where(member[:, s : s + 1] > 0.0, lse[s : s + 1], NEGATIVE))
    factor = jnp.exp(lse - exact_dot(slot_member, top))
    factor = jnp.where(owner >= 0.0, factor, 0.0)
    own_weight = jnp.exp(own - top)
    whole = exact_dot(member, factor) + own_weight
    slot_whole = exact_dot(slot_member, whole)
    slot_part = factor / jnp.where(owner >= 0.0, slot_whole, 1.0)
    own_part = own_weight / whole
    parts = jnp.concatenate([slot_part, own_part], axis=0)

    for copy in sum_copies:
        copy.wait_recv()
    slot_sums = sums[...].astype(jnp.float32).reshape(HOLDERS, REPEAT, slots, PLANE)
    member = member.astype(jnp.bfloat16)
    spread_head = head_of((128, PLANE), 1)
    spread_row = lax.broadcasted_iota(jnp.int32, (128, PLANE), 0)
    results = []
    for k in range(REPEAT):
        expand = jnp.where(spread_row == spread_head + k * KV_HEADS, 1.0, 0.0)
        shares = split_dot(parts, expand.astype(jnp.bfloat16))
        weighted = (shares[:every] * slot_sums[:, k].reshape(every, PLANE)).astype(jnp.bfloat16)
        results.append(
            jnp.dot(member, weighted, preferred_element_type=jnp.float32)
            + shares[every:] * new_values
        )
    attended[...] = jnp.concatenate(
        [
            results[k][:, g * HEAD_DIM : (g + 1) * HEAD_DIM]
            for g in range(KV_HEADS)
            for k in range(REPEAT)
        ],
        axis=1,
    ).astype(jnp.bfloat16)

    for copy in page_copies:
        copy.wait_recv()
    kept.wait()
    for copy in (
        list(moved.values()) + page_copies + proj_copies + query_copies + fresh_copies
        + peak_copies + sum_copies
    ):
        copy.wait_send()


def deliver_kernel(attended, compacted, attended_out, compacted_out, sems):
    copies = []
    for source, target, pieces in ((attended, attended_out, 2), (compacted, compacted_out, 4)):
        size = source.shape[0] // pieces
        for n in range(pieces):
            piece = pl.ds(n * size, size)
            copies.append(
                pltpu.make_async_copy(source.at[piece], target.at[piece], sems.at[len(copies)])
            )
    for copy in copies:
        copy.start()
    for copy in copies:
        copy.wait()


def fused_device(
    tokens, norm_gain, w_query, w_keyvalue, cache, page_count, page_owner, keep_rows, dest_slot
):
    slots, _, page_rows, width = cache.shape
    keep = keep_rows.shape[2]
    requests, model = tokens.shape
    part = requests // HOLDERS
    vmem = pl.BlockSpec(memory_space=pltpu.VMEM)
    pinned = pl.BlockSpec(memory_space=pltpu.HBM)
    bf16, f32 = jnp.bfloat16, jnp.float32
    dma = pltpu.SemaphoreType.DMA
    attended, compacted = pl.pallas_call(
        fused_kernel,
        out_shape=(
            jax.ShapeDtypeStruct((requests, HEADS * HEAD_DIM), bf16),
            jax.ShapeDtypeStruct((slots, keep, width), bf16),
        ),
        in_specs=[pinned] * 9,
        out_specs=(vmem, vmem),
        scratch_shapes=[
            pltpu.VMEM((part, model), bf16),
            pltpu.VMEM((model // 128, 128), f32),
            pltpu.VMEM((1, 1), jnp.int32),
            pltpu.VMEM((1, slots), jnp.int32),
            pltpu.VMEM((1, slots), jnp.int32),
            pltpu.VMEM(keep_rows.shape, jnp.int32),
            pltpu.VMEM((512, model), bf16),
            pltpu.VMEM((slots * page_rows, width), bf16),
            pltpu.VMEM((2, GROUPS, part, model // 2), bf16),
            pltpu.VMEM((slots, keep, width), bf16),
            pltpu.VMEM((GROUPS, part, 512), bf16),
            pltpu.VMEM((GROUPS, part, 512), bf16),
            pltpu.VMEM((HOLDERS, REPEAT, part, PLANE), bf16),
            pltpu.VMEM((HOLDERS, 2, part, PLANE), bf16),
            pltpu.VMEM((HOLDERS, REPEAT * slots, PLANE), bf16),
            pltpu.VMEM((HOLDERS, slots, 128), f32),
            dma((9,)),
            dma,
            dma((2, GROUPS)),
            dma((2, GROUPS)),
            dma((HOLDERS,)),
            dma((HOLDERS,)),
            dma((GROUPS,)),
            dma((GROUPS,)),
        ]
        + [dma((HOLDERS,))] * 8,
        compiler_params=pltpu.CompilerParams(
            collective_id=0, has_side_effects=True, vmem_limit_bytes=60 * 1024 * 1024
        ),
        cost_estimate=pl.CostEstimate(
            flops=1_500_000_000, bytes_accessed=7_000_000, transcendentals=70_000
        ),
    )(
        tokens.reshape(HOLDERS, part, model),
        norm_gain.reshape(model // 128, 128),
        page_count,
        page_owner.reshape(1, slots),
        dest_slot.reshape(1, slots),
        keep_rows,
        w_query.T,
        w_keyvalue.T,
        cache.reshape(slots * page_rows, width),
    )
    attended, compacted = pl.pallas_call(
        deliver_kernel,
        out_shape=(
            jax.ShapeDtypeStruct(attended.shape, bf16),
            jax.ShapeDtypeStruct(compacted.shape, bf16),
        ),
        in_specs=[pinned] * 2,
        out_specs=(pinned, pinned),
        scratch_shapes=[dma((6,))],
        compiler_params=pltpu.CompilerParams(vmem_limit_bytes=60 * 1024 * 1024),
        cost_estimate=pl.CostEstimate(flops=0, bytes_accessed=1_966_080, transcendentals=0),
    )(attended, compacted)
    return attended, compacted[:, None]


def local_step(sizes, tokens, norm_gain, w_query, w_keyvalue, cache, *rest):
    fits = (
        sizes == {"page": HOLDERS, "tensor": GROUPS}
        and tokens.shape[0] == 64
        and cache.shape[0] == 8
        and rest[2].shape[2] == 32
    )
    step = fused_device if fits else per_device
    return step(tokens, norm_gain, w_query, w_keyvalue, cache, *rest)


def solution(mesh):
    return jax.shard_map(
        functools.partial(local_step, dict(mesh.shape)),
        mesh=mesh,
        in_specs=(
            P("tensor", None),
            P(),
            P(None, "tensor"),
            P(None, "tensor"),
            P("page", "tensor", None, None),
            P("page", "tensor"),
            P("page", "tensor"),
            P("page", "tensor", None),
            P("page", "tensor"),
        ),
        out_specs=(P("tensor", None), P("page", "tensor", None, None)),
        check_vma=False,
    )
```

```python
import functools

import jax
import jax.numpy as jnp
from jax import lax
from jax.experimental import pallas as pl
from jax.experimental.pallas import tpu as pltpu
from jax.sharding import PartitionSpec as P

HEADS = 32
KV_HEADS = 8
HEAD_DIM = 80


EPSILON = 1e-05
NEGATIVE = -1e30


def per_device(
    tokens, norm_gain, w_query, w_keyvalue, cache, page_count, page_owner, keep_rows, dest_slot
):
    holders = lax.axis_size("page")
    groups = lax.axis_size("tensor")
    rows_here = tokens.shape[0]
    sources = cache.shape[0]
    keep_count = keep_rows.shape[2]
    row_width = cache.shape[3]
    capacity = (sources + holders - 1) // holders
    targets = capacity * holders
    repeat_count = HEADS // KV_HEADS
    score_scale = HEAD_DIM ** (-0.5)
    widened = tokens.astype(jnp.float32)
    normed = (
        widened
        * lax.rsqrt(jnp.mean(widened * widened, axis=-1, keepdims=True) + EPSILON)
        * norm_gain
    ).astype(jnp.bfloat16)
    portion = lax.all_gather(normed, "tensor", axis=0, tiled=True)
    query_part = jnp.dot(portion, w_query, preferred_element_type=jnp.float32)
    pair_part = jnp.dot(portion, w_keyvalue, preferred_element_type=jnp.float32)
    projected = jnp.concatenate([query_part, pair_part], axis=1).astype(jnp.bfloat16)
    local_heads = lax.all_to_all(
        projected, "tensor", split_axis=0, concat_axis=1, tiled=True
    ).reshape(rows_here, groups, -1)
    query_cols = w_query.shape[1]
    queries = local_heads[:, :, :query_cols].reshape(rows_here, KV_HEADS, repeat_count, HEAD_DIM)
    fresh_kv = local_heads[:, :, query_cols:].reshape(rows_here, 2, KV_HEADS, HEAD_DIM)
    new_keys = fresh_kv[:, 0]
    new_values = fresh_kv[:, 1]
    retained = jax.vmap(lambda one_page, row_picks: one_page[row_picks])(
        cache[:, 0], keep_rows[:, 0]
    )
    is_live = jnp.arange(sources) < page_count[0, 0]
    owners = page_owner[:, 0]
    chosen = (dest_slot[:, 0][None, :] == jnp.arange(targets)[:, None]) & is_live[None, :]
    outgoing = jnp.einsum(
        "ts,sjc->tjc", chosen.astype(jnp.bfloat16), retained, preferred_element_type=jnp.float32
    ).astype(jnp.bfloat16)
    out_tags = jnp.sum(jnp.where(chosen, owners[None, :] + 1, 0), axis=1) - 1
    arrived, arrived_tags = (
        lax.all_to_all(
            outgoing.reshape(holders, capacity, keep_count, row_width),
            "page",
            split_axis=0,
            concat_axis=0,
            tiled=True,
        ),
        lax.all_to_all(
            out_tags.reshape(holders, capacity), "page", split_axis=0, concat_axis=0, tiled=True
        ),
    )
    arrived = arrived.reshape(targets, keep_count, row_width)
    arrived_tags = arrived_tags.reshape(targets)
    slot_count = arrived.shape[0]
    active = arrived_tags >= 0
    owner_idx = jnp.maximum(arrived_tags, 0)
    picked = jnp.take(queries, owner_idx, axis=0)
    slot_keys = arrived[:, :, : KV_HEADS * HEAD_DIM].reshape(
        slot_count, keep_count, KV_HEADS, HEAD_DIM
    )
    slot_values = arrived[:, :, KV_HEADS * HEAD_DIM :].reshape(
        slot_count, keep_count, KV_HEADS, HEAD_DIM
    )
    scores = (
        jnp.einsum("sgkd,sjgd->sgkj", picked, slot_keys, preferred_element_type=jnp.float32)
        * score_scale
    )
    member = (owner_idx[None, :] == jnp.arange(rows_here)[:, None]) & active[None, :]
    slot_peak = jnp.max(scores, axis=3)
    local_peak = jnp.max(jnp.where(member[:, :, None, None], slot_peak[None], NEGATIVE), axis=1)
    own_score = (
        jnp.einsum("rgkd,rgd->rgk", queries, new_keys, preferred_element_type=jnp.float32)
        * score_scale
    )
    row_peak = jnp.maximum(lax.pmax(local_peak, "page"), own_score)
    shifted = scores - jnp.take(row_peak, owner_idx, axis=0)[..., None]
    weights = jnp.where(active[:, None, None, None], jnp.exp(shifted), 0.0)
    slot_total = jnp.sum(weights, axis=3)
    slot_out = jnp.einsum(
        "sgkj,sjgd->sgkd",
        weights.astype(jnp.bfloat16),
        slot_values,
        preferred_element_type=jnp.float32,
    )
    member_weight = member.astype(jnp.float32)
    part_total = jnp.einsum(
        "rs,sgk->rgk", member_weight, slot_total, precision=lax.Precision.HIGHEST
    )
    part_out = jnp.einsum("rs,sgkd->rgkd", member_weight, slot_out, precision=lax.Precision.HIGHEST)
    sum_out, sum_total = lax.psum((part_out, part_total), "page")
    own_weight = jnp.exp(own_score - row_peak)
    mixed = sum_out + own_weight[..., None] * new_values[:, :, None, :].astype(jnp.float32)
    result = mixed / (sum_total + own_weight)[..., None]
    return (result.reshape(rows_here, HEADS * HEAD_DIM).astype(jnp.bfloat16), arrived[:, None])


MESH = pl.DeviceIdType.MESH
SCALE = HEAD_DIM ** (-0.5)
REPEAT = HEADS // KV_HEADS
PLANE = KV_HEADS * HEAD_DIM
HOLDERS, GROUPS = 4, 8


def head_of(shape, axis):
    return (lax.broadcasted_iota(jnp.int32, shape, axis) * 3277) >> 18


def partner(index, flip):
    for bit in (1, 2, 4):
        if flip & bit:
            index = index + bit - 2 * bit * lax.rem(lax.div(index, bit), 2)
    return index


def split_dot(a, b):
    high = a.astype(jnp.bfloat16)
    low = (a - high.astype(jnp.float32)).astype(jnp.bfloat16)
    return jnp.dot(high, b, preferred_element_type=jnp.float32) + jnp.dot(
        low, b, preferred_element_type=jnp.float32
    )


def exact_dot(a, b):
    return jnp.dot(a, b, precision=lax.Precision.HIGHEST, preferred_element_type=jnp.float32)


def fused_kernel(
    tokens_in, gain_in, count_in, owners_in, targets_in, kept_in, w_query, w_keyvalue, cache,
    attended, compacted,
    tokens, gain, count, owners, targets, kept_rows, weight, pages, rows, leaving, projected, local, planes, fresh, sums, peaks,
    load_sem, keep_sem, row_send, row_recv, page_send, page_recv, proj_send, proj_recv,
    query_send, query_recv, fresh_send, fresh_recv, sum_send, sum_recv, peak_send, peak_recv,
):
    p = lax.axis_index("page")
    t = lax.axis_index("tensor")
    part = rows.shape[2]
    requests = part * HOLDERS
    slots = leaving.shape[0]
    keep = leaving.shape[1]
    cap = slots // HOLDERS
    page_rows = cache.shape[0] // slots

    loads = [
        pltpu.make_async_copy(tokens_in.at[p], tokens, load_sem.at[3]),
        pltpu.make_async_copy(gain_in, gain, load_sem.at[4]),
        pltpu.make_async_copy(count_in, count, load_sem.at[5]),
        pltpu.make_async_copy(owners_in, owners, load_sem.at[6]),
        pltpu.make_async_copy(targets_in, targets, load_sem.at[7]),
        pltpu.make_async_copy(kept_in, kept_rows, load_sem.at[8]),
        pltpu.make_async_copy(cache, pages, load_sem.at[0]),
        pltpu.make_async_copy(w_query, weight.at[pl.ds(0, 320)], load_sem.at[1]),
        pltpu.make_async_copy(w_keyvalue, weight.at[pl.ds(320, 160)], load_sem.at[2]),
    ]
    for load in loads:
        load.start()

    barrier = pltpu.get_barrier_semaphore()
    for f in range(1, GROUPS):
        pl.semaphore_signal(barrier, inc=1, device_id=(p, partner(t, f)), device_id_type=MESH)
    for f in range(1, HOLDERS):
        pl.semaphore_signal(barrier, inc=1, device_id=(partner(p, f), t), device_id_type=MESH)

    weight[480:512] = jnp.zeros((32, weight.shape[1]), weight.dtype)
    loads[0].wait()
    loads[1].wait()
    gains = gain[...]
    gains = jnp.concatenate([gains[i : i + 1] for i in range(gains.shape[0])], axis=1)
    mine = tokens[...].astype(jnp.float32)
    square = jnp.mean(mine * mine, axis=-1, keepdims=True)
    normed = (mine * lax.rsqrt(square + EPSILON) * gains).astype(jnp.bfloat16)
    half = normed.shape[1] // 2
    rows[0, 0] = normed[:, :half]
    rows[1, 0] = normed[:, half:]
    pl.semaphore_wait(barrier, GROUPS + HOLDERS - 2)

    def pass_row(h, e, f):
        copy = pltpu.make_async_remote_copy(
            src_ref=rows.at[h, e],
            dst_ref=rows.at[h, e ^ f],
            send_sem=row_send.at[h, e ^ f],
            recv_sem=row_recv.at[h, e ^ f],
            device_id=(p, partner(t, f)),
            device_id_type=MESH,
        )
        copy.start()
        return copy

    moved = {}
    for h in range(2):
        for f in (4, 2, 1):
            moved[h, f] = pass_row(h, 0, f)

    def forward(h, e):
        moved[h, e].wait_recv()
        if e == 4:
            moved[h, 6] = pass_row(h, 4, 2)
        if (h, e) == (1, 5):
            moved[h, 7] = pass_row(h, 5, 2)
        elif (h, e) != (1, 6):
            moved[h, e + 1] = pass_row(h, e, 1)

    for load in loads[2:6]:
        load.wait()
    live = lax.broadcasted_iota(jnp.int32, (1, slots), 1) < count[...]
    target = jnp.where(live, targets[...], -1)
    owner_plus = owners[...].astype(jnp.float32) + 1.0

    def tags_of(shape, shift):
        at = lax.broadcasted_iota(jnp.int32, shape, 0) >> shift
        return jnp.sum(jnp.where(target == at, owner_plus, 0.0), axis=1, keepdims=True) - 1.0

    pairs = slots * KV_HEADS
    tags = tags_of((slots, slots), 0)
    tag_rows = tags_of((pairs, slots), 3)
    picks = jnp.concatenate([kept_rows[s] for s in range(slots)], axis=0).astype(jnp.float32)
    placed = (slots * keep, keep)
    repeat_rows = jnp.where(
        (lax.broadcasted_iota(jnp.int32, placed, 0) & (keep - 1))
        == lax.broadcasted_iota(jnp.int32, placed, 1),
        1.0,
        0.0,
    )
    code = lax.dot_general(
        repeat_rows.astype(jnp.bfloat16),
        picks.astype(jnp.bfloat16),
        (((1,), (1,)), ((), ())),
        preferred_element_type=jnp.float32,
    )
    at = lax.broadcasted_iota(jnp.int32, (slots * keep, slots), 0) >> 5
    code = jnp.where(target == at, code, -1.0)
    lane = lax.broadcasted_iota(jnp.int32, (slots * keep, page_rows), 1).astype(jnp.float32)
    choice = jnp.concatenate(
        [jnp.where(code[:, s : s + 1] == lane, 1.0, 0.0).astype(jnp.bfloat16) for s in range(slots)],
        axis=1,
    )
    loads[6].wait()
    forward(0, 4)
    forward(0, 2)
    left = jnp.dot(choice, pages[:, :PLANE], preferred_element_type=jnp.float32)
    forward(1, 4)
    forward(1, 2)
    right = jnp.dot(choice, pages[:, PLANE:], preferred_element_type=jnp.float32)
    out = jnp.concatenate([left, right], axis=1).astype(jnp.bfloat16)
    leaving[...] = out.reshape(leaving.shape)
    page_copies = []
    for f in range(1, HOLDERS):
        copy = pltpu.make_async_remote_copy(
            src_ref=leaving.at[pl.ds(partner(p, f) * cap, cap)],
            dst_ref=compacted.at[pl.ds(p * cap, cap)],
            send_sem=page_send.at[f],
            recv_sem=page_recv.at[f],
            device_id=(partner(p, f), t),
            device_id_type=MESH,
        )
        copy.start()
        page_copies.append(copy)
    kept = pltpu.make_async_copy(
        leaving.at[pl.ds(p * cap, cap)], compacted.at[pl.ds(p * cap, cap)], keep_sem
    )
    kept.start()

    loads[7].wait()
    loads[8].wait()
    forward(0, 6)
    forward(1, 5)
    forward(1, 6)

    def project(first):
        both = 0.0
        for h in range(2):
            if first == 1:
                for e in (1, 3, 5, 7):
                    if (h, e) != (1, 5):
                        moved[h, e].wait_recv()
            both += lax.dot_general(
                jnp.concatenate([rows[h, e] for e in range(first, GROUPS, 2)], axis=0),
                weight[:, h * half : (h + 1) * half],
                (((1,), (1,)), ((), ())),
                preferred_element_type=jnp.float32,
            )
        both = both.astype(jnp.bfloat16)
        copies = []
        for n, e in enumerate(range(first, GROUPS, 2)):
            block = both[n * part : (n + 1) * part]
            if e == 0:
                local[t] = block
                continue
            projected[e] = block
            copy = pltpu.make_async_remote_copy(
                src_ref=projected.at[e],
                dst_ref=local.at[t],
                send_sem=proj_send.at[e],
                recv_sem=proj_recv.at[e],
                device_id=(p, partner(t, e)),
                device_id_type=MESH,
            )
            copy.start()
            copies.append(copy)
        return copies

    proj_copies = project(0)
    proj_copies += project(1)
    for copy in proj_copies:
        copy.wait_recv()

    blocks = [local[g].astype(jnp.float32) for g in range(GROUPS)]
    for k in range(REPEAT):
        planes[p, k] = jnp.concatenate(
            [b[:, k * HEAD_DIM : (k + 1) * HEAD_DIM] for b in blocks], axis=1
        ).astype(jnp.bfloat16)
    for n in range(2):
        fresh[p, n] = jnp.concatenate(
            [b[:, 320:480] for b in blocks[4 * n : 4 * n + 4]], axis=1
        ).astype(jnp.bfloat16)

    def to_holders(ref_of, send, recv):
        copies = []
        for f in range(1, HOLDERS):
            copy = pltpu.make_async_remote_copy(
                src_ref=ref_of(),
                dst_ref=ref_of(),
                send_sem=send.at[f],
                recv_sem=recv.at[f],
                device_id=(partner(p, f), t),
                device_id_type=MESH,
            )
            copy.start()
            copies.append(copy)
        return copies

    query_copies = to_holders(lambda: planes.at[p], query_send, query_recv)
    fresh_copies = to_holders(lambda: fresh.at[p], fresh_send, fresh_recv)

    def plane(ref, k):
        return jnp.concatenate([ref[h, k] for h in range(HOLDERS)], axis=0)

    member_row = jnp.where(
        tag_rows == lax.broadcasted_iota(jnp.int32, (pairs, requests), 1).astype(jnp.float32),
        1.0,
        0.0,
    ).astype(jnp.bfloat16)
    own_head = head_of((pairs, PLANE), 1) == (
        lax.broadcasted_iota(jnp.int32, (pairs, PLANE), 0) & (KV_HEADS - 1)
    )
    slot_rows = leaving[...].reshape(slots * keep, 2 * PLANE)
    for copy in query_copies:
        copy.wait_recv()

    spread = []
    for k in range(REPEAT):
        q = plane(planes, k)
        found = jnp.dot(member_row, q, preferred_element_type=jnp.float32)
        spread.append(jnp.where(own_head, found, 0.0).astype(jnp.bfloat16))
    scores = SCALE * lax.dot_general(
        jnp.concatenate(spread, axis=0),
        slot_rows[:, :PLANE],
        (((1,), (1,)), ((), ())),
        preferred_element_type=jnp.float32,
    )
    full = (REPEAT * pairs, slots * keep)
    same = ((lax.broadcasted_iota(jnp.int32, full, 0) >> 3) & (slots - 1)) == (
        lax.broadcasted_iota(jnp.int32, full, 1) >> 5
    )
    scores = jnp.where(same, scores, NEGATIVE)
    peak = jnp.max(scores, axis=1, keepdims=True)
    weights = jnp.where(same, jnp.exp(scores - peak), 0.0)
    total = jnp.sum(weights, axis=1, keepdims=True)
    mixed = jnp.dot(
        weights.astype(jnp.bfloat16), slot_rows[:, PLANE:], preferred_element_type=jnp.float32
    ) * (1.0 / total)
    mixed = mixed.reshape(REPEAT, pairs, PLANE)
    mixed = jnp.where(own_head[None], mixed, 0.0).astype(jnp.bfloat16)
    gather = (REPEAT * slots, REPEAT * pairs)
    of_slot = lax.broadcasted_iota(jnp.int32, gather, 0) == (
        lax.broadcasted_iota(jnp.int32, gather, 1) >> 3
    )
    sums[p] = jnp.dot(
        jnp.where(of_slot, 1.0, 0.0).astype(jnp.bfloat16),
        mixed.reshape(REPEAT * pairs, PLANE),
        preferred_element_type=jnp.float32,
    ).astype(jnp.bfloat16)
    lse = peak + jnp.log(total)
    wide = (REPEAT * pairs, 128)
    row_id = lax.broadcasted_iota(jnp.int32, wide, 0)
    at = (row_id >> 6) * KV_HEADS + (row_id & (KV_HEADS - 1))
    lse = jnp.where(lax.broadcasted_iota(jnp.int32, wide, 1) == at, lse, 0.0)
    lse = jnp.sum(lse.reshape(REPEAT, slots, KV_HEADS, 128), axis=2)
    lse = lse[0] + lse[1] + lse[2] + lse[3]
    peaks[p] = jnp.where(
        lax.broadcasted_iota(jnp.int32, (slots, 128), 1) == 127, tags, lse
    )
    peak_copies = to_holders(lambda: peaks.at[p], peak_send, peak_recv)
    sum_copies = to_holders(lambda: sums.at[p], sum_send, sum_recv)

    for copy in fresh_copies:
        copy.wait_recv()
    new_keys = plane(fresh, 0).astype(jnp.float32)
    new_values = plane(fresh, 1).astype(jnp.float32)
    own = jnp.zeros((requests, 128), jnp.float32)
    segment_head = head_of((PLANE, 128), 0)
    segment_lane = lax.broadcasted_iota(jnp.int32, (PLANE, 128), 1)
    for k in range(REPEAT):
        q = plane(planes, k).astype(jnp.float32)
        segment = jnp.where(segment_lane == segment_head + k * KV_HEADS, 1.0, 0.0)
        own += split_dot(q * new_keys, segment.astype(jnp.bfloat16))
    own = own * SCALE

    for copy in peak_copies:
        copy.wait_recv()
    every = HOLDERS * slots
    lse = peaks[...].reshape(every, 128)
    owner = lse[:, 127:128]
    where_slot = lax.broadcasted_iota(jnp.int32, (every, every), 0)
    where_lane = lax.broadcasted_iota(jnp.int32, (every, every), 1)
    owner_row = jnp.sum(jnp.where(where_slot == where_lane, owner, 0.0), axis=0, keepdims=True)
    request = lax.broadcasted_iota(jnp.int32, (requests, every), 0).astype(jnp.float32)
    member = jnp.where(request == owner_row, 1.0, 0.0)
    request = lax.broadcasted_iota(jnp.int32, (every, requests), 1).astype(jnp.float32)
    slot_member = jnp.where(request == owner, 1.0, 0.0)
    top = own
    for s in range(every):
        top = jnp.maximum(top, jnp.where(member[:, s : s + 1] > 0.0, lse[s : s + 1], NEGATIVE))
    factor = jnp.exp(lse - exact_dot(slot_member, top))
    factor = jnp.where(owner >= 0.0, factor, 0.0)
    own_weight = jnp.exp(own - top)
    whole = exact_dot(member, factor) + own_weight
    slot_whole = exact_dot(slot_member, whole)
    slot_part = factor / jnp.where(owner >= 0.0, slot_whole, 1.0)
    own_part = own_weight / whole
    parts = jnp.concatenate([slot_part, own_part], axis=0)

    for copy in sum_copies:
        copy.wait_recv()
    slot_sums = sums[...].astype(jnp.float32).reshape(HOLDERS, REPEAT, slots, PLANE)
    member = member.astype(jnp.bfloat16)
    spread_head = head_of((128, PLANE), 1)
    spread_row = lax.broadcasted_iota(jnp.int32, (128, PLANE), 0)
    results = []
    for k in range(REPEAT):
        expand = jnp.where(spread_row == spread_head + k * KV_HEADS, 1.0, 0.0)
        shares = split_dot(parts, expand.astype(jnp.bfloat16))
        weighted = (shares[:every] * slot_sums[:, k].reshape(every, PLANE)).astype(jnp.bfloat16)
        results.append(
            jnp.dot(member, weighted, preferred_element_type=jnp.float32)
            + shares[every:] * new_values
        )
    attended[...] = jnp.concatenate(
        [
            results[k][:, g * HEAD_DIM : (g + 1) * HEAD_DIM]
            for g in range(KV_HEADS)
            for k in range(REPEAT)
        ],
        axis=1,
    ).astype(jnp.bfloat16)

    for copy in page_copies:
        copy.wait_recv()
    kept.wait()
    for copy in (
        list(moved.values()) + page_copies + proj_copies + query_copies + fresh_copies
        + peak_copies + sum_copies
    ):
        copy.wait_send()


def deliver_kernel(attended, compacted, attended_out, compacted_out, rows, pages, get, put):
    fetches, copies = [], []
    ways = ((attended, rows, attended_out, 2), (compacted, pages, compacted_out, 4))
    for source, middle, target, pieces in ways:
        size = source.shape[0] // pieces
        for n in range(pieces):
            piece = pl.ds(n * size, size)
            at = len(copies)
            fetches.append(pltpu.make_async_copy(source.at[piece], middle.at[piece], get.at[at]))
            copies.append(pltpu.make_async_copy(middle.at[piece], target.at[piece], put.at[at]))
    for fetch in fetches:
        fetch.start()
    for fetch, copy in zip(fetches, copies):
        fetch.wait()
        copy.start()
    for copy in copies:
        copy.wait()


def fused_device(
    tokens, norm_gain, w_query, w_keyvalue, cache, page_count, page_owner, keep_rows, dest_slot
):
    slots, _, page_rows, width = cache.shape
    keep = keep_rows.shape[2]
    requests, model = tokens.shape
    part = requests // HOLDERS
    vmem = pl.BlockSpec(memory_space=pltpu.VMEM)
    pinned = pl.BlockSpec(memory_space=pltpu.HBM)
    bf16, f32 = jnp.bfloat16, jnp.float32
    dma = pltpu.SemaphoreType.DMA
    attended, compacted = pl.pallas_call(
        fused_kernel,
        out_shape=(
            jax.ShapeDtypeStruct((requests, HEADS * HEAD_DIM), bf16),
            jax.ShapeDtypeStruct((slots, keep, width), bf16),
        ),
        in_specs=[pinned] * 9,
        out_specs=(vmem, vmem),
        scratch_shapes=[
            pltpu.VMEM((part, model), bf16),
            pltpu.VMEM((model // 128, 128), f32),
            pltpu.VMEM((1, 1), jnp.int32),
            pltpu.VMEM((1, slots), jnp.int32),
            pltpu.VMEM((1, slots), jnp.int32),
            pltpu.VMEM(keep_rows.shape, jnp.int32),
            pltpu.VMEM((512, model), bf16),
            pltpu.VMEM((slots * page_rows, width), bf16),
            pltpu.VMEM((2, GROUPS, part, model // 2), bf16),
            pltpu.VMEM((slots, keep, width), bf16),
            pltpu.VMEM((GROUPS, part, 512), bf16),
            pltpu.VMEM((GROUPS, part, 512), bf16),
            pltpu.VMEM((HOLDERS, REPEAT, part, PLANE), bf16),
            pltpu.VMEM((HOLDERS, 2, part, PLANE), bf16),
            pltpu.VMEM((HOLDERS, REPEAT * slots, PLANE), bf16),
            pltpu.VMEM((HOLDERS, slots, 128), f32),
            dma((9,)),
            dma,
            dma((2, GROUPS)),
            dma((2, GROUPS)),
            dma((HOLDERS,)),
            dma((HOLDERS,)),
            dma((GROUPS,)),
            dma((GROUPS,)),
        ]
        + [dma((HOLDERS,))] * 8,
        compiler_params=pltpu.CompilerParams(
            collective_id=0, has_side_effects=True, vmem_limit_bytes=60 * 1024 * 1024
        ),
        cost_estimate=pl.CostEstimate(
            flops=1_500_000_000, bytes_accessed=7_000_000, transcendentals=70_000
        ),
    )(
        tokens.reshape(HOLDERS, part, model),
        norm_gain.reshape(model // 128, 128),
        page_count,
        page_owner.reshape(1, slots),
        dest_slot.reshape(1, slots),
        keep_rows,
        w_query.T,
        w_keyvalue.T,
        cache.reshape(slots * page_rows, width),
    )
    attended, compacted = pl.pallas_call(
        deliver_kernel,
        out_shape=(
            jax.ShapeDtypeStruct(attended.shape, bf16),
            jax.ShapeDtypeStruct(compacted.shape, bf16),
        ),
        in_specs=[pinned] * 2,
        out_specs=(pinned, pinned),
        scratch_shapes=[
            pltpu.VMEM(attended.shape, bf16),
            pltpu.VMEM(compacted.shape, bf16),
            dma((6,)),
            dma((6,)),
        ],
        compiler_params=pltpu.CompilerParams(vmem_limit_bytes=60 * 1024 * 1024),
        cost_estimate=pl.CostEstimate(flops=0, bytes_accessed=1_966_080, transcendentals=0),
    )(attended, compacted)
    return attended, compacted[:, None]


def local_step(sizes, tokens, norm_gain, w_query, w_keyvalue, cache, *rest):
    fits = (
        sizes == {"page": HOLDERS, "tensor": GROUPS}
        and tokens.shape[0] == 64
        and cache.shape[0] == 8
        and rest[2].shape[2] == 32
    )
    step = fused_device if fits else per_device
    return step(tokens, norm_gain, w_query, w_keyvalue, cache, *rest)


def solution(mesh):
    return jax.shard_map(
        functools.partial(local_step, dict(mesh.shape)),
        mesh=mesh,
        in_specs=(
            P("tensor", None),
            P(),
            P(None, "tensor"),
            P(None, "tensor"),
            P("page", "tensor", None, None),
            P("page", "tensor"),
            P("page", "tensor"),
            P("page", "tensor", None),
            P("page", "tensor"),
        ),
        out_specs=(P("tensor", None), P("page", "tensor", None, None)),
        check_vma=False,
    )
```

```python
import functools

import jax
import jax.numpy as jnp
from jax import lax
from jax.experimental import pallas as pl
from jax.experimental.pallas import tpu as pltpu
from jax.sharding import PartitionSpec as P

HEADS = 32
KV_HEADS = 8
HEAD_DIM = 80


EPSILON = 1e-05
NEGATIVE = -1e30


def per_device(
    tokens, norm_gain, w_query, w_keyvalue, cache, page_count, page_owner, keep_rows, dest_slot
):
    holders = lax.axis_size("page")
    groups = lax.axis_size("tensor")
    rows_here = tokens.shape[0]
    sources = cache.shape[0]
    keep_count = keep_rows.shape[2]
    row_width = cache.shape[3]
    capacity = (sources + holders - 1) // holders
    targets = capacity * holders
    repeat_count = HEADS // KV_HEADS
    score_scale = HEAD_DIM ** (-0.5)
    widened = tokens.astype(jnp.float32)
    normed = (
        widened
        * lax.rsqrt(jnp.mean(widened * widened, axis=-1, keepdims=True) + EPSILON)
        * norm_gain
    ).astype(jnp.bfloat16)
    portion = lax.all_gather(normed, "tensor", axis=0, tiled=True)
    query_part = jnp.dot(portion, w_query, preferred_element_type=jnp.float32)
    pair_part = jnp.dot(portion, w_keyvalue, preferred_element_type=jnp.float32)
    projected = jnp.concatenate([query_part, pair_part], axis=1).astype(jnp.bfloat16)
    local_heads = lax.all_to_all(
        projected, "tensor", split_axis=0, concat_axis=1, tiled=True
    ).reshape(rows_here, groups, -1)
    query_cols = w_query.shape[1]
    queries = local_heads[:, :, :query_cols].reshape(rows_here, KV_HEADS, repeat_count, HEAD_DIM)
    fresh_kv = local_heads[:, :, query_cols:].reshape(rows_here, 2, KV_HEADS, HEAD_DIM)
    new_keys = fresh_kv[:, 0]
    new_values = fresh_kv[:, 1]
    retained = jax.vmap(lambda one_page, row_picks: one_page[row_picks])(
        cache[:, 0], keep_rows[:, 0]
    )
    is_live = jnp.arange(sources) < page_count[0, 0]
    owners = page_owner[:, 0]
    chosen = (dest_slot[:, 0][None, :] == jnp.arange(targets)[:, None]) & is_live[None, :]
    outgoing = jnp.einsum(
        "ts,sjc->tjc", chosen.astype(jnp.bfloat16), retained, preferred_element_type=jnp.float32
    ).astype(jnp.bfloat16)
    out_tags = jnp.sum(jnp.where(chosen, owners[None, :] + 1, 0), axis=1) - 1
    arrived, arrived_tags = (
        lax.all_to_all(
            outgoing.reshape(holders, capacity, keep_count, row_width),
            "page",
            split_axis=0,
            concat_axis=0,
            tiled=True,
        ),
        lax.all_to_all(
            out_tags.reshape(holders, capacity), "page", split_axis=0, concat_axis=0, tiled=True
        ),
    )
    arrived = arrived.reshape(targets, keep_count, row_width)
    arrived_tags = arrived_tags.reshape(targets)
    slot_count = arrived.shape[0]
    active = arrived_tags >= 0
    owner_idx = jnp.maximum(arrived_tags, 0)
    picked = jnp.take(queries, owner_idx, axis=0)
    slot_keys = arrived[:, :, : KV_HEADS * HEAD_DIM].reshape(
        slot_count, keep_count, KV_HEADS, HEAD_DIM
    )
    slot_values = arrived[:, :, KV_HEADS * HEAD_DIM :].reshape(
        slot_count, keep_count, KV_HEADS, HEAD_DIM
    )
    scores = (
        jnp.einsum("sgkd,sjgd->sgkj", picked, slot_keys, preferred_element_type=jnp.float32)
        * score_scale
    )
    member = (owner_idx[None, :] == jnp.arange(rows_here)[:, None]) & active[None, :]
    slot_peak = jnp.max(scores, axis=3)
    local_peak = jnp.max(jnp.where(member[:, :, None, None], slot_peak[None], NEGATIVE), axis=1)
    own_score = (
        jnp.einsum("rgkd,rgd->rgk", queries, new_keys, preferred_element_type=jnp.float32)
        * score_scale
    )
    row_peak = jnp.maximum(lax.pmax(local_peak, "page"), own_score)
    shifted = scores - jnp.take(row_peak, owner_idx, axis=0)[..., None]
    weights = jnp.where(active[:, None, None, None], jnp.exp(shifted), 0.0)
    slot_total = jnp.sum(weights, axis=3)
    slot_out = jnp.einsum(
        "sgkj,sjgd->sgkd",
        weights.astype(jnp.bfloat16),
        slot_values,
        preferred_element_type=jnp.float32,
    )
    member_weight = member.astype(jnp.float32)
    part_total = jnp.einsum(
        "rs,sgk->rgk", member_weight, slot_total, precision=lax.Precision.HIGHEST
    )
    part_out = jnp.einsum("rs,sgkd->rgkd", member_weight, slot_out, precision=lax.Precision.HIGHEST)
    sum_out, sum_total = lax.psum((part_out, part_total), "page")
    own_weight = jnp.exp(own_score - row_peak)
    mixed = sum_out + own_weight[..., None] * new_values[:, :, None, :].astype(jnp.float32)
    result = mixed / (sum_total + own_weight)[..., None]
    return (result.reshape(rows_here, HEADS * HEAD_DIM).astype(jnp.bfloat16), arrived[:, None])


MESH = pl.DeviceIdType.MESH
SCALE = HEAD_DIM ** (-0.5)
REPEAT = HEADS // KV_HEADS
PLANE = KV_HEADS * HEAD_DIM
HOLDERS, GROUPS = 4, 8


def head_of(shape, axis):
    return (lax.broadcasted_iota(jnp.int32, shape, axis) * 3277) >> 18


def partner(index, flip):
    for bit in (1, 2, 4):
        if flip & bit:
            index = index + bit - 2 * bit * lax.rem(lax.div(index, bit), 2)
    return index


def split_dot(a, b):
    high = a.astype(jnp.bfloat16)
    low = (a - high.astype(jnp.float32)).astype(jnp.bfloat16)
    return jnp.dot(high, b, preferred_element_type=jnp.float32) + jnp.dot(
        low, b, preferred_element_type=jnp.float32
    )


def exact_dot(a, b):
    return jnp.dot(a, b, precision=lax.Precision.HIGHEST, preferred_element_type=jnp.float32)


def fused_kernel(
    tokens_in, gain_in, count_in, owners_in, targets_in, kept_in, w_query, w_keyvalue, cache,
    attended, compacted,
    tokens, gain, count, owners, targets, kept_rows, weight, pages, rows, leaving, projected, local, planes, fresh, sums, peaks,
    load_sem, keep_sem, row_send, row_recv, page_send, page_recv, proj_send, proj_recv,
    query_send, query_recv, fresh_send, fresh_recv, sum_send, sum_recv, peak_send, peak_recv,
):
    p = lax.axis_index("page")
    t = lax.axis_index("tensor")
    part = rows.shape[2]
    requests = part * HOLDERS
    slots = leaving.shape[0]
    keep = leaving.shape[1]
    cap = slots // HOLDERS
    page_rows = cache.shape[0] // slots

    loads = [
        pltpu.make_async_copy(tokens_in.at[p], tokens, load_sem.at[3]),
        pltpu.make_async_copy(gain_in, gain, load_sem.at[4]),
        pltpu.make_async_copy(count_in, count, load_sem.at[5]),
        pltpu.make_async_copy(owners_in, owners, load_sem.at[6]),
        pltpu.make_async_copy(targets_in, targets, load_sem.at[7]),
        pltpu.make_async_copy(kept_in, kept_rows, load_sem.at[8]),
        pltpu.make_async_copy(cache, pages, load_sem.at[0]),
        pltpu.make_async_copy(w_query, weight.at[pl.ds(0, 320)], load_sem.at[1]),
        pltpu.make_async_copy(w_keyvalue, weight.at[pl.ds(320, 160)], load_sem.at[2]),
    ]
    for load in loads:
        load.start()

    barrier = pltpu.get_barrier_semaphore()
    for f in range(1, GROUPS):
        pl.semaphore_signal(barrier, inc=1, device_id=(p, partner(t, f)), device_id_type=MESH)
    for f in range(1, HOLDERS):
        pl.semaphore_signal(barrier, inc=1, device_id=(partner(p, f), t), device_id_type=MESH)

    weight[480:512] = jnp.zeros((32, weight.shape[1]), weight.dtype)
    loads[0].wait()
    loads[1].wait()
    gains = gain[...]
    gains = jnp.concatenate([gains[i : i + 1] for i in range(gains.shape[0])], axis=1)
    mine = tokens[...].astype(jnp.float32)
    square = jnp.mean(mine * mine, axis=-1, keepdims=True)
    normed = (mine * lax.rsqrt(square + EPSILON) * gains).astype(jnp.bfloat16)
    half = normed.shape[1] // 2
    rows[0, 0] = normed[:, :half]
    rows[1, 0] = normed[:, half:]
    pl.semaphore_wait(barrier, GROUPS + HOLDERS - 2)

    def pass_row(h, e, f):
        copy = pltpu.make_async_remote_copy(
            src_ref=rows.at[h, e],
            dst_ref=rows.at[h, e ^ f],
            send_sem=row_send.at[h, e ^ f],
            recv_sem=row_recv.at[h, e ^ f],
            device_id=(p, partner(t, f)),
            device_id_type=MESH,
        )
        copy.start()
        return copy

    moved = {}
    for h in range(2):
        for f in (4, 2, 1):
            moved[h, f] = pass_row(h, 0, f)

    def forward(h, e):
        moved[h, e].wait_recv()
        if e == 4:
            moved[h, 6] = pass_row(h, 4, 2)
        if (h, e) == (1, 5):
            moved[h, 7] = pass_row(h, 5, 2)
        elif (h, e) != (1, 6):
            moved[h, e + 1] = pass_row(h, e, 1)

    for load in loads[2:6]:
        load.wait()
    live = lax.broadcasted_iota(jnp.int32, (1, slots), 1) < count[...]
    target = jnp.where(live, targets[...], -1)
    owner_plus = owners[...].astype(jnp.float32) + 1.0

    def tags_of(shape, shift):
        at = lax.broadcasted_iota(jnp.int32, shape, 0) >> shift
        return jnp.sum(jnp.where(target == at, owner_plus, 0.0), axis=1, keepdims=True) - 1.0

    pairs = slots * KV_HEADS
    tags = tags_of((slots, slots), 0)
    tag_rows = tags_of((pairs, slots), 3)
    picks = jnp.concatenate([kept_rows[s] for s in range(slots)], axis=0).astype(jnp.float32)
    placed = (slots * keep, keep)
    repeat_rows = jnp.where(
        (lax.broadcasted_iota(jnp.int32, placed, 0) & (keep - 1))
        == lax.broadcasted_iota(jnp.int32, placed, 1),
        1.0,
        0.0,
    )
    code = lax.dot_general(
        repeat_rows.astype(jnp.bfloat16),
        picks.astype(jnp.bfloat16),
        (((1,), (1,)), ((), ())),
        preferred_element_type=jnp.float32,
    )
    at = lax.broadcasted_iota(jnp.int32, (slots * keep, slots), 0) >> 5
    code = jnp.where(target == at, code, -1.0)
    lane = lax.broadcasted_iota(jnp.int32, (slots * keep, page_rows), 1).astype(jnp.float32)
    choice = jnp.concatenate(
        [jnp.where(code[:, s : s + 1] == lane, 1.0, 0.0).astype(jnp.bfloat16) for s in range(slots)],
        axis=1,
    )
    loads[6].wait()
    forward(0, 4)
    forward(0, 2)
    left = jnp.dot(choice, pages[:, :PLANE], preferred_element_type=jnp.float32)
    forward(1, 4)
    forward(1, 2)
    right = jnp.dot(choice, pages[:, PLANE:], preferred_element_type=jnp.float32)
    out = jnp.concatenate([left, right], axis=1).astype(jnp.bfloat16)
    leaving[...] = out.reshape(leaving.shape)
    page_copies = []
    for f in range(1, HOLDERS):
        copy = pltpu.make_async_remote_copy(
            src_ref=leaving.at[pl.ds(partner(p, f) * cap, cap)],
            dst_ref=compacted.at[pl.ds(p * cap, cap)],
            send_sem=page_send.at[f],
            recv_sem=page_recv.at[f],
            device_id=(partner(p, f), t),
            device_id_type=MESH,
        )
        copy.start()
        page_copies.append(copy)
    kept = pltpu.make_async_copy(
        leaving.at[pl.ds(p * cap, cap)], compacted.at[pl.ds(p * cap, cap)], keep_sem
    )
    kept.start()

    loads[7].wait()
    loads[8].wait()
    forward(0, 6)
    forward(1, 5)
    forward(1, 6)

    def project(first):
        both = 0.0
        for h in range(2):
            if first == 1:
                for e in (1, 3, 5, 7):
                    if (h, e) != (1, 5):
                        moved[h, e].wait_recv()
            both += lax.dot_general(
                jnp.concatenate([rows[h, e] for e in range(first, GROUPS, 2)], axis=0),
                weight[:, h * half : (h + 1) * half],
                (((1,), (1,)), ((), ())),
                preferred_element_type=jnp.float32,
            )
        both = both.astype(jnp.bfloat16)
        copies = []
        for n, e in enumerate(range(first, GROUPS, 2)):
            block = both[n * part : (n + 1) * part]
            if e == 0:
                local[t] = block
                continue
            projected[e] = block
            copy = pltpu.make_async_remote_copy(
                src_ref=projected.at[e],
                dst_ref=local.at[t],
                send_sem=proj_send.at[e],
                recv_sem=proj_recv.at[e],
                device_id=(p, partner(t, e)),
                device_id_type=MESH,
            )
            copy.start()
            copies.append(copy)
        return copies

    proj_copies = project(0)
    proj_copies += project(1)
    for copy in proj_copies:
        copy.wait_recv()

    blocks = [local[g].astype(jnp.float32) for g in range(GROUPS)]
    for k in range(REPEAT):
        planes[p, k] = jnp.concatenate(
            [b[:, k * HEAD_DIM : (k + 1) * HEAD_DIM] for b in blocks], axis=1
        ).astype(jnp.bfloat16)
    for n in range(2):
        fresh[p, n] = jnp.concatenate(
            [b[:, 320:480] for b in blocks[4 * n : 4 * n + 4]], axis=1
        ).astype(jnp.bfloat16)

    def to_holders(ref_of, send, recv, flips=(1, 2, 3)):
        copies = []
        for f in flips:
            copy = pltpu.make_async_remote_copy(
                src_ref=ref_of(),
                dst_ref=ref_of(),
                send_sem=send.at[f],
                recv_sem=recv.at[f],
                device_id=(partner(p, f), t),
                device_id_type=MESH,
            )
            copy.start()
            copies.append(copy)
        return copies

    query_copies = to_holders(lambda: planes.at[p], query_send, query_recv, (2, 1))
    fresh_copies = to_holders(lambda: fresh.at[p], fresh_send, fresh_recv)

    def plane(ref, k):
        return jnp.concatenate([ref[h, k] for h in range(HOLDERS)], axis=0)

    member_row = jnp.where(
        tag_rows == lax.broadcasted_iota(jnp.int32, (pairs, requests), 1).astype(jnp.float32),
        1.0,
        0.0,
    ).astype(jnp.bfloat16)
    own_head = head_of((pairs, PLANE), 1) == (
        lax.broadcasted_iota(jnp.int32, (pairs, PLANE), 0) & (KV_HEADS - 1)
    )
    slot_rows = leaving[...].reshape(slots * keep, 2 * PLANE)
    query_copies[0].wait_recv()
    beyond = planes.at[partner(p, 2)]
    query_copies.append(
        pltpu.make_async_remote_copy(
            src_ref=beyond,
            dst_ref=beyond,
            send_sem=query_send.at[3],
            recv_sem=query_recv.at[3],
            device_id=(partner(p, 1), t),
            device_id_type=MESH,
        )
    )
    query_copies[2].start()
    for copy in query_copies[1:]:
        copy.wait_recv()

    spread = []
    for k in range(REPEAT):
        q = plane(planes, k)
        found = jnp.dot(member_row, q, preferred_element_type=jnp.float32)
        spread.append(jnp.where(own_head, found, 0.0).astype(jnp.bfloat16))
    scores = SCALE * lax.dot_general(
        jnp.concatenate(spread, axis=0),
        slot_rows[:, :PLANE],
        (((1,), (1,)), ((), ())),
        preferred_element_type=jnp.float32,
    )
    full = (REPEAT * pairs, slots * keep)
    same = ((lax.broadcasted_iota(jnp.int32, full, 0) >> 3) & (slots - 1)) == (
        lax.broadcasted_iota(jnp.int32, full, 1) >> 5
    )
    scores = jnp.where(same, scores, NEGATIVE)
    peak = jnp.max(scores, axis=1, keepdims=True)
    weights = jnp.where(same, jnp.exp(scores - peak), 0.0)
    total = jnp.sum(weights, axis=1, keepdims=True)
    mixed = jnp.dot(
        weights.astype(jnp.bfloat16), slot_rows[:, PLANE:], preferred_element_type=jnp.float32
    ) * (1.0 / total)
    mixed = mixed.reshape(REPEAT, pairs, PLANE)
    mixed = jnp.where(own_head[None], mixed, 0.0).astype(jnp.bfloat16)
    gather = (REPEAT * slots, REPEAT * pairs)
    of_slot = lax.broadcasted_iota(jnp.int32, gather, 0) == (
        lax.broadcasted_iota(jnp.int32, gather, 1) >> 3
    )
    sums[p] = jnp.dot(
        jnp.where(of_slot, 1.0, 0.0).astype(jnp.bfloat16),
        mixed.reshape(REPEAT * pairs, PLANE),
        preferred_element_type=jnp.float32,
    ).astype(jnp.bfloat16)
    lse = peak + jnp.log(total)
    wide = (REPEAT * pairs, 128)
    row_id = lax.broadcasted_iota(jnp.int32, wide, 0)
    at = (row_id >> 6) * KV_HEADS + (row_id & (KV_HEADS - 1))
    lse = jnp.where(lax.broadcasted_iota(jnp.int32, wide, 1) == at, lse, 0.0)
    lse = jnp.sum(lse.reshape(REPEAT, slots, KV_HEADS, 128), axis=2)
    lse = lse[0] + lse[1] + lse[2] + lse[3]
    peaks[p] = jnp.where(
        lax.broadcasted_iota(jnp.int32, (slots, 128), 1) == 127, tags, lse
    )
    peak_copies = to_holders(lambda: peaks.at[p], peak_send, peak_recv)
    sum_copies = to_holders(lambda: sums.at[p], sum_send, sum_recv)

    for copy in fresh_copies:
        copy.wait_recv()
    new_keys = plane(fresh, 0).astype(jnp.float32)
    new_values = plane(fresh, 1).astype(jnp.float32)
    own = jnp.zeros((requests, 128), jnp.float32)
    segment_head = head_of((PLANE, 128), 0)
    segment_lane = lax.broadcasted_iota(jnp.int32, (PLANE, 128), 1)
    for k in range(REPEAT):
        q = plane(planes, k).astype(jnp.float32)
        segment = jnp.where(segment_lane == segment_head + k * KV_HEADS, 1.0, 0.0)
        own += split_dot(q * new_keys, segment.astype(jnp.bfloat16))
    own = own * SCALE

    for copy in peak_copies:
        copy.wait_recv()
    every = HOLDERS * slots
    lse = peaks[...].reshape(every, 128)
    owner = lse[:, 127:128]
    where_slot = lax.broadcasted_iota(jnp.int32, (every, every), 0)
    where_lane = lax.broadcasted_iota(jnp.int32, (every, every), 1)
    owner_row = jnp.sum(jnp.where(where_slot == where_lane, owner, 0.0), axis=0, keepdims=True)
    request = lax.broadcasted_iota(jnp.int32, (requests, every), 0).astype(jnp.float32)
    member = jnp.where(request == owner_row, 1.0, 0.0)
    request = lax.broadcasted_iota(jnp.int32, (every, requests), 1).astype(jnp.float32)
    slot_member = jnp.where(request == owner, 1.0, 0.0)
    top = own
    for s in range(every):
        top = jnp.maximum(top, jnp.where(member[:, s : s + 1] > 0.0, lse[s : s + 1], NEGATIVE))
    factor = jnp.exp(lse - exact_dot(slot_member, top))
    factor = jnp.where(owner >= 0.0, factor, 0.0)
    own_weight = jnp.exp(own - top)
    whole = exact_dot(member, factor) + own_weight
    slot_whole = exact_dot(slot_member, whole)
    slot_part = factor / jnp.where(owner >= 0.0, slot_whole, 1.0)
    own_part = own_weight / whole
    parts = jnp.concatenate([slot_part, own_part], axis=0)

    for copy in sum_copies:
        copy.wait_recv()
    slot_sums = sums[...].astype(jnp.float32).reshape(HOLDERS, REPEAT, slots, PLANE)
    member = member.astype(jnp.bfloat16)
    spread_head = head_of((128, PLANE), 1)
    spread_row = lax.broadcasted_iota(jnp.int32, (128, PLANE), 0)
    results = []
    for k in range(REPEAT):
        expand = jnp.where(spread_row == spread_head + k * KV_HEADS, 1.0, 0.0)
        shares = split_dot(parts, expand.astype(jnp.bfloat16))
        weighted = (shares[:every] * slot_sums[:, k].reshape(every, PLANE)).astype(jnp.bfloat16)
        results.append(
            jnp.dot(member, weighted, preferred_element_type=jnp.float32)
            + shares[every:] * new_values
        )
    attended[...] = jnp.concatenate(
        [
            results[k][:, g * HEAD_DIM : (g + 1) * HEAD_DIM]
            for g in range(KV_HEADS)
            for k in range(REPEAT)
        ],
        axis=1,
    ).astype(jnp.bfloat16)

    for copy in page_copies:
        copy.wait_recv()
    kept.wait()
    for copy in (
        list(moved.values()) + page_copies + proj_copies + query_copies + fresh_copies
        + peak_copies + sum_copies
    ):
        copy.wait_send()


def deliver_kernel(attended, compacted, attended_out, compacted_out, rows, pages, get, put):
    fetches, copies = [], []
    ways = ((attended, rows, attended_out, 2), (compacted, pages, compacted_out, 4))
    for source, middle, target, pieces in ways:
        size = source.shape[0] // pieces
        for n in range(pieces):
            piece = pl.ds(n * size, size)
            at = len(copies)
            fetches.append(pltpu.make_async_copy(source.at[piece], middle.at[piece], get.at[at]))
            copies.append(pltpu.make_async_copy(middle.at[piece], target.at[piece], put.at[at]))
    for fetch in fetches:
        fetch.start()
    for fetch, copy in zip(fetches, copies):
        fetch.wait()
        copy.start()
    for copy in copies:
        copy.wait()


def fused_device(
    tokens, norm_gain, w_query, w_keyvalue, cache, page_count, page_owner, keep_rows, dest_slot
):
    slots, _, page_rows, width = cache.shape
    keep = keep_rows.shape[2]
    requests, model = tokens.shape
    part = requests // HOLDERS
    vmem = pl.BlockSpec(memory_space=pltpu.VMEM)
    pinned = pl.BlockSpec(memory_space=pltpu.HBM)
    bf16, f32 = jnp.bfloat16, jnp.float32
    dma = pltpu.SemaphoreType.DMA
    attended, compacted = pl.pallas_call(
        fused_kernel,
        out_shape=(
            jax.ShapeDtypeStruct((requests, HEADS * HEAD_DIM), bf16),
            jax.ShapeDtypeStruct((slots, keep, width), bf16),
        ),
        in_specs=[pinned] * 9,
        out_specs=(vmem, pl.BlockSpec(memory_space=pl.ANY)),
        scratch_shapes=[
            pltpu.VMEM((part, model), bf16),
            pltpu.VMEM((model // 128, 128), f32),
            pltpu.VMEM((1, 1), jnp.int32),
            pltpu.VMEM((1, slots), jnp.int32),
            pltpu.VMEM((1, slots), jnp.int32),
            pltpu.VMEM(keep_rows.shape, jnp.int32),
            pltpu.VMEM((512, model), bf16),
            pltpu.VMEM((slots * page_rows, width), bf16),
            pltpu.VMEM((2, GROUPS, part, model // 2), bf16),
            pltpu.VMEM((slots, keep, width), bf16),
            pltpu.VMEM((GROUPS, part, 512), bf16),
            pltpu.VMEM((GROUPS, part, 512), bf16),
            pltpu.VMEM((HOLDERS, REPEAT, part, PLANE), bf16),
            pltpu.VMEM((HOLDERS, 2, part, PLANE), bf16),
            pltpu.VMEM((HOLDERS, REPEAT * slots, PLANE), bf16),
            pltpu.VMEM((HOLDERS, slots, 128), f32),
            dma((9,)),
            dma,
            dma((2, GROUPS)),
            dma((2, GROUPS)),
            dma((HOLDERS,)),
            dma((HOLDERS,)),
            dma((GROUPS,)),
            dma((GROUPS,)),
        ]
        + [dma((HOLDERS,))] * 8,
        compiler_params=pltpu.CompilerParams(
            collective_id=0, has_side_effects=True, vmem_limit_bytes=60 * 1024 * 1024
        ),
        cost_estimate=pl.CostEstimate(
            flops=1_500_000_000, bytes_accessed=7_000_000, transcendentals=70_000
        ),
    )(
        tokens.reshape(HOLDERS, part, model),
        norm_gain.reshape(model // 128, 128),
        page_count,
        page_owner.reshape(1, slots),
        dest_slot.reshape(1, slots),
        keep_rows,
        w_query.T,
        w_keyvalue.T,
        cache.reshape(slots * page_rows, width),
    )
    attended, compacted = pl.pallas_call(
        deliver_kernel,
        out_shape=(
            jax.ShapeDtypeStruct(attended.shape, bf16),
            jax.ShapeDtypeStruct(compacted.shape, bf16),
        ),
        in_specs=[pinned] * 2,
        out_specs=(pinned, pinned),
        scratch_shapes=[
            pltpu.VMEM(attended.shape, bf16),
            pltpu.VMEM(compacted.shape, bf16),
            dma((6,)),
            dma((6,)),
        ],
        compiler_params=pltpu.CompilerParams(vmem_limit_bytes=60 * 1024 * 1024),
        cost_estimate=pl.CostEstimate(flops=0, bytes_accessed=1_966_080, transcendentals=0),
    )(attended, compacted)
    return attended, compacted[:, None]


def local_step(sizes, tokens, norm_gain, w_query, w_keyvalue, cache, *rest):
    fits = (
        sizes == {"page": HOLDERS, "tensor": GROUPS}
        and tokens.shape[0] == 64
        and cache.shape[0] == 8
        and rest[2].shape[2] == 32
    )
    step = fused_device if fits else per_device
    return step(tokens, norm_gain, w_query, w_keyvalue, cache, *rest)


def solution(mesh):
    return jax.shard_map(
        functools.partial(local_step, dict(mesh.shape)),
        mesh=mesh,
        in_specs=(
            P("tensor", None),
            P(),
            P(None, "tensor"),
            P(None, "tensor"),
            P("page", "tensor", None, None),
            P("page", "tensor"),
            P("page", "tensor"),
            P("page", "tensor", None),
            P("page", "tensor"),
        ),
        out_specs=(P("tensor", None), P("page", "tensor", None, None)),
        check_vma=False,
    )
```
